128 devices in a mesh: row: 4 (over y_hi, core), col: 4 (over z), chan: 8 (over x, y_lo).
Axes of the slice: x: 4, y: 4 (y_hi: 2, y_lo: 2; y = y_hi * 2 + y_lo), z: 4, core: 2. Of those that a mesh axis runs over, the one named last changes fastest.
Arguments:
- feature_map: bfloat16 [512, 64, 512], P('chan', 'row', 'col'), may hold values from -6 to 6
- base_kernel: float32 [512, 5, 5], P('chan'), may hold values from -1.25 to 1.25
- base_bias: float32 [512], P('chan'), may hold values from -3 to 3
- base_scale: float32 [512], P('chan'), may hold values from 0.3 to 3
- wave_kernels: float32 [3, 512, 4, 5, 5], P(None, 'chan'), may hold values from -1.25 to 1.25
- wave_scale: float32 [3, 512, 4], P(None, 'chan'), may hold values from 0.3 to 1
- norm_gain: float32 [512], P('chan'), may hold values from 0.5 to 2
- norm_bias: float32 [512], P('chan'), may hold values from -3 to 3
- w_in: bfloat16 [512, 2048], P(None, 'chan'), may hold values from -0.25 to 0.25
- b_in: float32 [2048], P('chan'), may hold values from -3 to 3
- w_out: bfloat16 [2048, 512], P('chan'), may hold values from -0.125 to 0.125
- b_out: float32 [512], P('chan'), may hold values from -3 to 3
- layer_scale: float32 [512], P('chan'), may hold values from 0.5 to 2
- cotangent: bfloat16 [512, 64, 512], P('chan', 'row', 'col'), may hold values from -6 to 6
Outputs:
- output_map: bfloat16 [512, 64, 512], P('chan', 'row', 'col')
- grad_map: bfloat16 [512, 64, 512], P('chan', 'row', 'col')
- grad_w_in: float32 [512, 2048], P(None, 'chan')
- grad_w_out: float32 [2048, 512], P('chan')
The draws below stay inside these ranges and needn't reach their ends.
All inputs are finite; a program needn't handle non-finite values.
Results may differ from the reference program's by a relative error of at most 0.028.
Values may be sent and summed in bfloat16 or wider, within the bound.
No kernel may reach another device: no remote copies, remote signals or barrier semaphores. Data moves between devices by JAX's collectives and lax.ppermute only.
A program may use at most 128 MiB of HBM per device.

```python
import math
import jax
import jax.numpy as jnp
from jax import lax

C = 512
HID = 2048
KERNEL = 5
LEVELS = 3
HT = 16
H = 64
W = 512
N_ROW = 4


def shard_levels(key, extent, split, least, largest):
    def one(dim, blocks):
        heights = jax.random.uniform(jax.random.fold_in(jax.random.fold_in(key, 6), dim), (blocks,), jnp.float32, least / len(split), largest / len(split))
        return jnp.repeat(jnp.exp(heights), extent[dim] // blocks).reshape((-1,) + (1,) * (len(extent) - dim - 1))

    factor_of = one(*split[0])
    for cut in split[1:]:
        factor_of = factor_of * one(*cut)
    return factor_of


def scatter_about(own_key, dims, spread, limit, split=(), held_as=jnp.bfloat16):
    values = spread * jax.random.normal(own_key, dims, jnp.float32)
    if split:
        values = values * shard_levels(own_key, dims, split, -0.22, 0.18)
    return jnp.clip(values, -limit, limit).astype(held_as)


def setup_inputs(seed: int = 0) -> dict:
    key_of = jax.random.split(jax.random.key(seed), 15)
    return {
        "feature_map": scatter_about(key_of[0], (C, H, W), 1.0, 6.0, ((0, 8), (1, 4), (2, 4))),
        "base_kernel": scatter_about(key_of[1], (C, KERNEL, KERNEL), (KERNEL * KERNEL) ** -0.5, 1.25, ((0, 8),), jnp.float32),
        "base_bias": scatter_about(key_of[2], (C,), 0.5, 3.0, ((0, 8),), jnp.float32),
        "base_scale": jnp.clip(jnp.exp(math.log(3.0) - 2.3025851 * jax.random.uniform(key_of[3], (C,), jnp.float32) ** shard_levels(key_of[3], (C,), ((0, 8),), -0.2, 0.2)), 0.3, 3.0),
        "wave_kernels": scatter_about(key_of[4], (LEVELS, C, 4, KERNEL, KERNEL), (KERNEL * KERNEL) ** -0.5, 1.25, ((1, 8),), jnp.float32),
        "wave_scale": jnp.clip(0.3 + 0.7 * jax.random.uniform(key_of[5], (LEVELS, C, 4), jnp.float32) ** shard_levels(key_of[5], (LEVELS, C, 4), ((1, 8),), -0.2, 0.2), 0.3, 1.0),
        "norm_gain": jnp.clip(jnp.exp(math.log(2.0) - 1.3862944 * jax.random.uniform(key_of[6], (C,), jnp.float32) ** shard_levels(key_of[6], (C,), ((0, 8),), -0.2, 0.2)), 0.5, 2.0),
        "norm_bias": scatter_about(key_of[7], (C,), 0.5, 3.0, ((0, 8),), jnp.float32),
        "w_in": scatter_about(key_of[8], (C, HID), C ** -0.5, 0.25, ((1, 8),)),
        "b_in": scatter_about(key_of[9], (HID,), 0.5, 3.0, ((0, 8),), jnp.float32),
        "w_out": scatter_about(key_of[10], (HID, C), HID ** -0.5, 0.125, ((0, 8),)),
        "b_out": scatter_about(key_of[11], (C,), 0.5, 3.0, ((0, 8),), jnp.float32),
        "layer_scale": jnp.clip(jnp.exp(math.log(2.0) - 1.3862944 * jax.random.uniform(key_of[12], (C,), jnp.float32) ** shard_levels(key_of[12], (C,), ((0, 8),), -0.2, 0.2)), 0.5, 2.0),
        "cotangent": scatter_about(key_of[13], (C, H, W), 1.0, 6.0, ((0, 8), (1, 4), (2, 4))),
    }


EPSILON = 1e-06
INV_ROOT_TWO = 0.7071067811865476
INV_ROOT_TWO_PI = 0.3989422804014327

def haar_split(source):
    shape_in = source.shape
    blocks = source.reshape(shape_in[:-2] + (shape_in[-2] // 2, 2, shape_in[-1] // 2, 2))
    upleft = blocks[..., :, 0, :, 0]
    upright = blocks[..., :, 0, :, 1]
    lowleft = blocks[..., :, 1, :, 0]
    lowright = blocks[..., :, 1, :, 1]
    return 0.5 * jnp.stack([upleft + upright + lowleft + lowright, upleft - upright + lowleft - lowright, upleft + upright - lowleft - lowright, upleft - upright - lowleft + lowright], axis=-3)

def haar_merge(subbands):
    coarse = subbands[..., 0, :, :]
    across = subbands[..., 1, :, :]
    downward = subbands[..., 2, :, :]
    diagonal = subbands[..., 3, :, :]
    upleft = 0.5 * (coarse + across + downward + diagonal)
    upright = 0.5 * (coarse - across + downward - diagonal)
    lowleft = 0.5 * (coarse + across - downward - diagonal)
    lowright = 0.5 * (coarse - across - downward + diagonal)
    blocks = jnp.stack([jnp.stack([upleft, upright], -1), jnp.stack([lowleft, lowright], -1)], -3)
    shape_in = blocks.shape
    return blocks.reshape(shape_in[:-4] + (shape_in[-4] * 2, shape_in[-2] * 2))

def depthwise(padded, kernel):
    rows_out = padded.shape[-2] - kernel.shape[-2] + 1
    cols_out = padded.shape[-1] - kernel.shape[-1] + 1
    summed = jnp.zeros(padded.shape[:-2] + (rows_out, cols_out), jnp.float32)
    for tap_row in range(kernel.shape[-2]):
        for tap_col in range(kernel.shape[-1]):
            summed = summed + kernel[..., tap_row, tap_col][..., None, None] * padded[..., tap_row:tap_row + rows_out, tap_col:tap_col + cols_out]
    return summed

def mirror(kernel):
    return kernel[..., ::-1, ::-1]

def wavelet_forward(source, base_kernel, base_bias, base_scale, wave_kernels, wave_scale, padder):
    lowpass = source
    branches = []
    for degree in range(wave_kernels.shape[0]):
        subbands = haar_split(lowpass)
        lowpass = subbands[:, 0]
        branches.append(wave_scale[degree][:, :, None, None] * depthwise(padder(subbands), wave_kernels[degree]))
    coarser = None
    for degree in reversed(range(wave_kernels.shape[0])):
        merged = branches[degree]
        if coarser is not None:
            merged = merged.at[:, 0].add(coarser)
        coarser = haar_merge(merged)
    based = depthwise(padder(source[:, None]), base_kernel[:, None])[:, 0]
    return base_scale[:, None, None] * (based + base_bias[:, None, None]) + coarser

def wavelet_backward(upstream, base_kernel, base_scale, wave_kernels, wave_scale, padder):
    result = depthwise(padder((base_scale[:, None, None] * upstream)[:, None]), mirror(base_kernel)[:, None])[:, 0]
    lowpass = upstream
    sources = []
    for degree in range(wave_kernels.shape[0]):
        subbands = haar_split(lowpass)
        lowpass = subbands[:, 0]
        sources.append(depthwise(padder(wave_scale[degree][:, :, None, None] * subbands), mirror(wave_kernels[degree])))
    carried = None
    for degree in reversed(range(wave_kernels.shape[0])):
        merged = sources[degree]
        if carried is not None:
            merged = merged.at[:, 0].add(carried)
        carried = haar_merge(merged)
    return result + carried

def zero_pad(source):
    return jnp.pad(source, ((0, 0), (0, 0), (2, 2), (2, 2)))

def gelu_slope(hidden):
    return 0.5 * (1.0 + lax.erf(hidden * INV_ROOT_TWO)) + hidden * jnp.exp(-0.5 * hidden * hidden) * INV_ROOT_TWO_PI

def mlp_block(mixed_rows, scaled, norm_gain, norm_bias, w_in, b_in, w_out, chan_count):
    values = mixed_rows.astype(jnp.float32)
    average = lax.optimization_barrier(jnp.sum(values, 0)) / chan_count
    rescale = lax.rsqrt(lax.optimization_barrier(jnp.sum(values * values, 0)) / chan_count - average * average + EPSILON)
    centred = (values - average) * rescale
    normed = (centred * norm_gain[:, None] + norm_bias[:, None]).astype(jnp.bfloat16)
    hidden = lax.dot_general(w_in, normed, (((0,), (0,)), ((), ())), preferred_element_type=jnp.float32) + b_in[:, None]
    activated = jax.nn.gelu(hidden, approximate=False).astype(jnp.bfloat16)
    projected = lax.dot_general(w_out, activated, (((0,), (0,)), ((), ())), preferred_element_type=jnp.float32)
    grad_activated = jnp.dot(w_out, scaled, preferred_element_type=jnp.float32)
    grad_hidden = (grad_activated * gelu_slope(hidden)).astype(jnp.bfloat16)
    part_out = lax.dot_general(activated, scaled, (((1,), (1,)), ((), ())), preferred_element_type=jnp.float32)
    part_in = lax.dot_general(normed, grad_hidden, (((1,), (1,)), ((), ())), preferred_element_type=jnp.float32)
    grad_normed = jnp.dot(w_in, grad_hidden, preferred_element_type=jnp.float32)
    weighted = grad_normed * norm_gain[:, None]
    grad_mixed = rescale * (weighted - lax.optimization_barrier(jnp.sum(weighted, 0)) / chan_count - centred * lax.optimization_barrier(jnp.sum(weighted * centred, 0)) / chan_count)
    return (projected, grad_mixed, part_in, part_out)

def reference(feature_map, base_kernel, base_bias, base_scale, wave_kernels, wave_scale, norm_gain, norm_bias, w_in, b_in, w_out, b_out, layer_scale, cotangent):
    source = feature_map.astype(jnp.float32)
    mixed_map = wavelet_forward(source, base_kernel, base_bias, base_scale, wave_kernels, wave_scale, zero_pad).astype(jnp.bfloat16)
    channels, height, width = feature_map.shape
    scaled = (layer_scale[:, None, None] * cotangent.astype(jnp.float32)).astype(jnp.bfloat16)

    def by_rows(array):
        return array.reshape(channels, N_ROW, HT * width).transpose(1, 0, 2)

    def from_rows(array):
        return array.transpose(1, 0, 2).reshape(channels, height, width)

    def scan_step(running, blocks):
        projected, grad_mixed, part_in, part_out = mlp_block(blocks[0], blocks[1], norm_gain, norm_bias, w_in, b_in, w_out, channels)
        return ((running[0] + part_in, running[1] + part_out), (projected, grad_mixed))
    start_sums = (jnp.zeros(w_in.shape, jnp.float32), jnp.zeros(w_out.shape, jnp.float32))
    sums, outputs = lax.scan(scan_step, start_sums, (by_rows(mixed_map), by_rows(scaled)))
    output_map = (source + layer_scale[:, None, None] * (from_rows(outputs[0]) + b_out[:, None, None])).astype(jnp.bfloat16)
    backward = wavelet_backward(from_rows(outputs[1]), base_kernel, base_scale, wave_kernels, wave_scale, zero_pad)
    grad_map = (cotangent.astype(jnp.float32) + backward).astype(jnp.bfloat16)
    grad_factor = 1.0 / float(height * width) ** 0.5
    return (output_map, grad_map, sums[0] * grad_factor, sums[1] * grad_factor)
```

```python
import jax
import jax.numpy as jnp
from jax import lax
from jax.experimental import pallas as pl
from jax.experimental.pallas import tpu as pltpu
from jax.sharding import Mesh, PartitionSpec as P

EPSILON = 1e-06
INV_ROOT_TWO = 0.7071067811865476
INV_ROOT_TWO_PI = 0.3989422804014327
F32 = jnp.float32
BF16 = jnp.bfloat16

CHANS = 512
PLANES = 4
HALVES = 2
SUB = PLANES * HALVES
ROWS = 32
COLS = 512
BAND = 256
SPOTS = HALVES * BAND
HID = 256
GROUP = 16
X = 4
Y = 2
VMEM_LIMIT = 48 * 1024 * 1024


def lanes(width=COLS):
    return lax.broadcasted_iota(jnp.int32, (SUB, width), 1)


def sublanes(width=COLS):
    return lax.broadcasted_iota(jnp.int32, (SUB, width), 0)


def turn(value, shift):
    return pltpu.roll(value, shift % value.shape[1], 1)


def pair_lanes(value, step, lane):
    return jnp.where((lane & step) == 0, value + turn(value, -step), turn(value, step) - value)


def fill_edges(ref, rows):
    low = sublanes() < PLANES
    for edge in range(2):
        ref[edge] = jnp.where(low, 0.0, pltpu.roll(ref[rows + edge], PLANES, 0))
        ref[rows + 2 + edge] = jnp.where(low, pltpu.roll(ref[2 + edge], PLANES, 0), 0.0)


def convolve(source, rows, step, taps, first, mirrored, shifted, target, start):
    lane = lanes()

    def shift_row(row, carry):
        value = source[row]
        for move in range(5):
            offset = (move - 2) * step
            if offset == 0:
                shifted[move, row] = value
            else:
                kept = (lane < COLS - offset) if offset > 0 else (lane >= -offset)
                shifted[move, row] = jnp.where(kept, turn(value, -offset), 0.0)
        return carry

    lax.fori_loop(0, rows + 4, shift_row, 0)
    chunk = min(rows, 8)

    def do_chunk(index, carry):
        base = index * chunk
        for block in range(COLS // 128):
            cols = slice(block * 128, block * 128 + 128)
            sums = [None] * chunk
            for move in range(5):
                coefs = []
                for tap_row in range(5):
                    place = tap_row * 5 + move
                    coefs.append(taps[first + (24 - place if mirrored else place)])
                for row in range(chunk + 4):
                    value = shifted[move, base + row, :, cols]
                    for tap_row in range(5):
                        out = row - tap_row
                        if 0 <= out < chunk:
                            term = coefs[tap_row] * value
                            sums[out] = term if sums[out] is None else sums[out] + term
            for row in range(chunk):
                target[start + base + row, :, cols] = sums[row]
        return carry

    lax.fori_loop(0, rows // chunk, do_chunk, 0)


def wavelet(plane, taps, mirrored, shifted, level_1, level_2, level_3, conv_0, conv_1, conv_2, conv_3):
    lane = lanes()
    fill_edges(plane, ROWS)

    def split_1(row, carry):
        upper, lower = plane[2 + 2 * row], plane[3 + 2 * row]
        level_1[0, 2 + row] = pair_lanes(0.5 * (upper + lower), 1, lane)
        level_1[1, 2 + row] = pair_lanes(0.5 * (upper - lower), 1, lane)
        return carry

    lax.fori_loop(0, ROWS // 2, split_1, 0)
    fill_edges(level_1.at[0], ROWS // 2)
    fill_edges(level_1.at[1], ROWS // 2)

    for source, target, rows, step in ((level_1.at[0], level_2, ROWS // 4, 2), (level_2, level_3, ROWS // 8, 4)):
        for row in range(rows):
            upper, lower = source[2 + 2 * row], source[3 + 2 * row]
            across = pair_lanes(0.5 * (upper + lower), step, lane)
            down = pair_lanes(0.5 * (upper - lower), step, lane)
            target[2 + row] = jnp.where((lane & (step - 1)) == 0, across, turn(down, 1))
        fill_edges(target, rows)

    convolve(plane, ROWS, 1, taps, 0, mirrored, shifted, conv_0, 0)
    convolve(level_1.at[0], ROWS // 2, 2, taps, 25, mirrored, shifted, conv_1.at[0], 0)
    convolve(level_1.at[1], ROWS // 2, 2, taps, 50, mirrored, shifted, conv_1.at[1], 0)
    convolve(level_2, ROWS // 4, 4, taps, 75, mirrored, shifted, conv_2, 0)
    convolve(level_3, ROWS // 8, 8, taps, 100, mirrored, shifted, conv_3, 0)

    for source, target, rows, step in ((conv_3, conv_2, ROWS // 8, 4), (conv_2, conv_1.at[0], ROWS // 4, 2)):
        for row in range(rows):
            kept = source[row]
            moved = turn(kept, -1)
            for half, value in ((0, kept + moved), (1, kept - moved)):
                merged = pair_lanes(0.5 * value, step, lane)
                place = 2 * row + half
                target[place] = target[place] + jnp.where((lane & (step - 1)) == 0, merged, 0.0)


def merged_rows(row, conv_1, lane):
    across, down = conv_1[0, row], conv_1[1, row]
    return pair_lanes(0.5 * (across + down), 1, lane), pair_lanes(0.5 * (across - down), 1, lane)


def tile_in(tiles, first, row_block, col):
    parts = [tiles[(2 * half + row_block) * 4 + col, first : first + PLANES].astype(F32) for half in range(HALVES)]
    return jnp.swapaxes(jnp.concatenate(parts, 0), 0, 1)


def forward_kernel(
    tiles, taps, shift, scale, sent, plane, shifted, level_1, level_2, level_3, conv_0, conv_1, conv_2, conv_3, second
):
    for row_block in range(2):
        for col in range(4):
            cols = slice(col * 128, col * 128 + 128)
            plane[2 + row_block * 16 : 18 + row_block * 16, :, cols] = tile_in(tiles, 0, row_block, col)
            second[row_block * 16 : 16 + row_block * 16, :, cols] = tile_in(tiles, PLANES, row_block, col)
    wavelet(plane, taps, False, shifted, level_1, level_2, level_3, conv_0, conv_1, conv_2, conv_3)
    lane = lanes()
    bias, layer = shift[...], scale[...]

    def finish(pair, carry):
        rows = merged_rows(pair, conv_1, lane)
        for half in range(2):
            row = 2 * pair + half
            mixed = conv_0[row] + bias + rows[half]
            scaled = layer * second[row]
            both = jnp.concatenate([mixed, scaled], 0).astype(BF16)
            for band in range(COLS // BAND):
                block = 2 * row + band
                part = both[:, band * BAND : band * BAND + BAND]
                for twin in range(Y):
                    sent[block // GROUP, twin, block % GROUP] = part
        return carry

    lax.fori_loop(0, ROWS // 2, finish, 0)


def backward_kernel(
    parts, tiles, taps, scale, shift, sent, plane, shifted, level_1, level_2, level_3, conv_0, conv_1, conv_2, conv_3, second
):
    def gather(block, carry):
        both = parts[block // GROUP, 0, block % GROUP].astype(F32) + parts[block // GROUP, 1, block % GROUP].astype(F32)
        cols = pl.ds(pl.multiple_of((block % 2) * BAND, BAND), BAND)
        second[block // 2, :, cols] = both[:SUB]
        plane[2 + block // 2, :, cols] = both[SUB:]
        return carry

    lax.fori_loop(0, 2 * ROWS, gather, 0)
    wavelet(plane, taps, True, shifted, level_1, level_2, level_3, conv_0, conv_1, conv_2, conv_3)
    lane = lanes()

    def finish(pair, carry):
        rows = merged_rows(pair, conv_1, lane)
        for half in range(2):
            row = 2 * pair + half
            conv_0[row] = conv_0[row] + rows[half]
        return carry

    lax.fori_loop(0, ROWS // 2, finish, 0)
    layer, bias = scale[...], shift[...]
    for row_block in range(2):
        for col in range(4):
            cols = slice(col * 128, col * 128 + 128)
            rows = slice(row_block * 16, row_block * 16 + 16)
            projected = layer[:, cols] * (second[rows, :, cols] + bias[:, cols])
            output = tile_in(tiles, 0, row_block, col) + projected
            grad = tile_in(tiles, PLANES, row_block, col) + conv_0[rows, :, cols]
            for first, value in ((0, output), (PLANES, grad)):
                turned = jnp.swapaxes(value, 0, 1).astype(BF16)
                for half in range(HALVES):
                    place = (2 * half + row_block) * 4 + col
                    sent[place, first : first + PLANES] = turned[half * PLANES : half * PLANES + PLANES]


def plane_scratch():
    return [
        pltpu.VMEM((ROWS + 4, SUB, COLS), F32),
        pltpu.VMEM((5, ROWS + 4, SUB, COLS), F32),
        pltpu.VMEM((2, ROWS // 2 + 4, SUB, COLS), F32),
        pltpu.VMEM((ROWS // 4 + 4, SUB, COLS), F32),
        pltpu.VMEM((ROWS // 8 + 4, SUB, COLS), F32),
        pltpu.VMEM((ROWS, SUB, COLS), F32),
        pltpu.VMEM((2, ROWS // 2, SUB, COLS), F32),
        pltpu.VMEM((ROWS // 4, SUB, COLS), F32),
        pltpu.VMEM((ROWS // 8, SUB, COLS), F32),
        pltpu.VMEM((ROWS, SUB, COLS), F32),
    ]


def regroup(first, second, low):
    return (
        jnp.where(low, first, pltpu.roll(second, PLANES, 0)),
        jnp.where(low, pltpu.roll(first, PLANES, 0), second),
    )


def dot(left, right, left_dim, right_dim):
    return lax.dot_general(left, right, (((left_dim,), (right_dim,)), ((), ())), preferred_element_type=F32)


def mlp_kernel(
    order, received, pack_0, pack_1, pack_2, pack_3, biases, gain, bias, sent, weight_sums, mixed, scaled, projected, grads
):
    low = sublanes(BAND) < PLANES

    def arrange(index, carry):
        rows = pl.ds(pl.multiple_of(index * 16, 16), 16)
        for half in range(HALVES):
            cols = slice(half * BAND, half * BAND + BAND)
            pieces = []
            for pair in range(2):
                one = received[4 * index + 2 * pair].astype(F32)
                two = received[4 * index + 2 * pair + 1].astype(F32)
                pieces.append((regroup(one[:SUB], two[:SUB], low)[half], regroup(one[SUB:], two[SUB:], low)[half]))
            mixed[rows, cols] = jnp.concatenate([pieces[0][0], pieces[1][0]], 0)
            scaled[rows, cols] = jnp.concatenate([pieces[0][1], pieces[1][1]], 0).astype(BF16)
        return carry

    lax.fori_loop(0, CHANS // 16, arrange, 0)
    values = mixed[...]
    average = jnp.sum(values, 0, keepdims=True) / CHANS
    rescale = lax.rsqrt(jnp.sum(values * values, 0, keepdims=True) / CHANS - average * average + EPSILON)
    gains = gain[...]
    normed = (((values - average) * rescale) * gains + bias[...]).astype(BF16)
    normed_turned = normed.T
    scaled_now = scaled[...]
    scaled_turned = scaled_now.T
    for index, pack in enumerate((pack_0, pack_1, pack_2, pack_3)):
        w_in, w_out = pack[:CHANS], pack[CHANS : 2 * CHANS]
        hidden = dot(normed_turned, w_in, 1, 0) + biases[index : index + 1]
        spread = 0.5 * (1.0 + lax.erf(hidden * INV_ROOT_TWO))
        activated = (hidden * spread).astype(BF16)
        slope = spread + hidden * jnp.exp(-0.5 * hidden * hidden) * INV_ROOT_TWO_PI
        grad_hidden = (dot(scaled_turned, w_out, 1, 0) * slope).astype(BF16)
        part = dot(w_out, activated, 1, 1)
        projected[...] = part if index == 0 else projected[...] + part
        part = dot(w_in, grad_hidden, 1, 1)
        grads[...] = part if index == 0 else grads[...] + part
        owner = order[0] ^ index
        for arr, value in ((0, dot(normed, grad_hidden, 1, 0)), (1, dot(scaled_now, activated, 1, 0))):
            rounded = value.astype(BF16)
            for piece in range(GROUP):
                weight_sums[owner, piece, arr] = rounded[piece * 32 : piece * 32 + 32]
    weighted = grads[...] * gains
    centred = (mixed[...] - average) * rescale
    sum_one = jnp.sum(weighted, 0, keepdims=True) / CHANS
    sum_two = jnp.sum(weighted * centred, 0, keepdims=True) / CHANS
    grads[...] = rescale * (weighted - sum_one - centred * sum_two)

    def hand_out(index, carry):
        rows = pl.ds(pl.multiple_of(index * 8, 8), 8)
        halves = []
        for ref in (projected, grads):
            value = ref[rows]
            halves.append(regroup(value[:, :BAND], value[:, BAND:], low))
        for place in range(2):
            sent[2 * index + place] = jnp.concatenate([halves[0][place], halves[1][place]], 0).astype(BF16)
        return carry

    lax.fori_loop(0, CHANS // 8, hand_out, 0)


def call(kernel, outs, scratch, ops, smem_first=False):
    spaces = [pl.BlockSpec(memory_space=pltpu.VMEM) for _ in ops]
    if smem_first:
        spaces[0] = pl.BlockSpec(memory_space=pltpu.SMEM)
    out_spaces = jax.tree.map(lambda _: pl.BlockSpec(memory_space=pltpu.VMEM), outs)
    return pl.pallas_call(
        kernel,
        out_shape=outs,
        in_specs=spaces,
        out_specs=out_spaces,
        scratch_shapes=scratch,
        compiler_params=pltpu.CompilerParams(vmem_limit_bytes=VMEM_LIMIT),
    )(*ops)


def three_parts(value):
    high = lax.reduce_precision(value, 8, 7)
    middle = lax.reduce_precision(value - high, 8, 7)
    return [part.astype(BF16) for part in (high, middle, value - high - middle)]


def own_planes(array, dim, place):
    return lax.dynamic_slice_in_dim(array, place * PLANES, PLANES, dim)


def over_halves(array):
    return jnp.concatenate([array, array], -2)


def tap_table(base_kernel, base_scale, wave_kernels, wave_scale):
    base = (base_scale[:, None, None] * base_kernel).reshape(PLANES, 25).T[:, :, None]
    waves = (wave_scale[..., None, None] * wave_kernels).reshape(3, PLANES, 4, 25).transpose(0, 2, 3, 1)[..., None]
    lane = jnp.arange(128)[None, None, :]

    def choose(level, period, bands):
        table = jnp.zeros((25, PLANES, 128), F32)
        for residue, band in bands:
            table = jnp.where(lane % period == residue, waves[level, band], table)
        return table

    tables = [
        jnp.broadcast_to(base, (25, PLANES, 128)),
        choose(0, 2, ((0, 0), (1, 1))),
        choose(0, 2, ((0, 2), (1, 3))),
        choose(1, 4, ((0, 0), (2, 1), (1, 2), (3, 3))),
        choose(2, 8, ((0, 0), (4, 1), (1, 2), (5, 3))),
    ]
    return over_halves(jnp.concatenate(tables, 0))


def on_device(
    feature_map,
    base_kernel,
    base_bias,
    base_scale,
    wave_kernels,
    wave_scale,
    norm_gain,
    norm_bias,
    w_in,
    b_in,
    w_out,
    b_out,
    layer_scale,
    cotangent,
):
    group = ("row", "col")
    everyone = ("x", "y", "row", "col")
    place = lax.axis_index("row") * 4 + lax.axis_index("col")
    x_here = lax.axis_index("x")
    y_here = lax.axis_index("y")

    norms = jnp.stack(three_parts(jnp.concatenate([norm_gain, norm_bias])))
    other = lax.ppermute(norms, "y", [(0, 1), (1, 0)])
    norms = jnp.concatenate([jnp.where(y_here == 0, norms, other), jnp.where(y_here == 0, other, norms)], 1)
    pack = jnp.concatenate(
        [w_in, w_out.T, jnp.stack(three_parts(b_in)), norms, jnp.zeros((10, HID), BF16)], 0
    )
    packs = [pack] + [lax.ppermute(pack, "x", [(i, i ^ step) for i in range(X)]) for step in range(1, X)]

    tiles = jnp.concatenate(
        [feature_map.reshape(GROUP, PLANES, 16, 128), cotangent.reshape(GROUP, PLANES, 16, 128)], 1
    )
    tiles = lax.all_to_all(tiles, group, split_axis=0, concat_axis=0, tiled=True)

    scale_own = own_planes(base_scale, 0, place)
    taps = tap_table(
        own_planes(base_kernel, 0, place),
        scale_own,
        own_planes(wave_kernels, 1, place),
        own_planes(wave_scale, 1, place),
    )

    def rows_of(vector):
        return over_halves(jnp.broadcast_to(vector[:, None], (PLANES, COLS)))

    layer = rows_of(own_planes(layer_scale, 0, place))
    sent = call(
        forward_kernel,
        jax.ShapeDtypeStruct((X, Y, GROUP, 2 * SUB, BAND), BF16),
        plane_scratch(),
        (tiles, taps, rows_of(scale_own * own_planes(base_bias, 0, place)), layer),
    )
    received = lax.all_to_all(
        sent.reshape(X * Y * GROUP, 2 * SUB, BAND), everyone, split_axis=0, concat_axis=0, tiled=True
    )

    extras = jnp.stack([one[2 * CHANS : 2 * CHANS + 6] for one in packs]).astype(F32)
    biases = extras[:, 0] + extras[:, 1] + extras[:, 2]
    vectors = (extras[:, 3] + extras[:, 4] + extras[:, 5])[x_here ^ jnp.arange(X)]
    vectors = vectors.reshape(X, Y, 2, CHANS // (X * Y)).transpose(2, 0, 1, 3).reshape(2, CHANS, 1)

    sent, weight_sums = call(
        mlp_kernel,
        (
            jax.ShapeDtypeStruct((X * Y * GROUP, 2 * SUB, BAND), BF16),
            jax.ShapeDtypeStruct((X, GROUP, 2, 32, HID), BF16),
        ),
        [
            pltpu.VMEM((CHANS, SPOTS), F32),
            pltpu.VMEM((CHANS, SPOTS), BF16),
            pltpu.VMEM((CHANS, SPOTS), F32),
            pltpu.VMEM((CHANS, SPOTS), F32),
        ],
        (x_here.astype(jnp.int32).reshape(1), received, *packs, biases, vectors[0], vectors[1]),
        smem_first=True,
    )
    received = lax.all_to_all(sent, everyone, split_axis=0, concat_axis=0, tiled=True)
    sent = call(
        backward_kernel,
        jax.ShapeDtypeStruct((GROUP, 2 * PLANES, 16, 128), BF16),
        plane_scratch(),
        (
            received.reshape(X, Y, GROUP, 2 * SUB, BAND),
            tiles,
            taps,
            layer,
            rows_of(own_planes(b_out, 0, place)),
        ),
    )
    results = lax.all_to_all(sent, group, split_axis=0, concat_axis=0, tiled=True)
    output_map = results[:, :PLANES].reshape(feature_map.shape)
    grad_map = results[:, PLANES:].reshape(feature_map.shape)

    pieces = lax.all_to_all(
        weight_sums.reshape(X * GROUP, 2, 32, HID), ("x", "row", "col"), split_axis=0, concat_axis=0, tiled=True
    )
    piece = jnp.sum(pieces.astype(F32), 0).astype(BF16)
    wholes = lax.all_to_all(
        jnp.broadcast_to(piece, (GROUP,) + piece.shape), group, split_axis=0, concat_axis=0, tiled=True
    )
    factor = 1.0 / (64.0 * 512.0) ** 0.5
    grad_in = wholes[:, 0].reshape(CHANS, HID).astype(F32) * factor
    grad_out = wholes[:, 1].reshape(CHANS, HID).T.astype(F32) * factor
    return (output_map, grad_map, grad_in, grad_out)


def solution(mesh):
    grid = Mesh(mesh.devices.reshape(4, 4, X, Y), ("row", "col", "x", "y"))
    chan = ("x", "y")
    return jax.shard_map(
        on_device,
        mesh=grid,
        in_specs=(
            P(chan, "row", "col"),
            P(chan, None, None),
            P(chan),
            P(chan),
            P(None, chan, None, None, None),
            P(None, chan, None),
            P(chan),
            P(chan),
            P(None, chan),
            P(chan),
            P(chan, None),
            P(chan),
            P(chan),
            P(chan, "row", "col"),
        ),
        out_specs=(
            P(chan, "row", "col"),
            P(chan, "row", "col"),
            P(None, chan),
            P(chan, None),
        ),
        check_vma=False,
    )
```

```python
import jax
import jax.numpy as jnp
from jax import lax
from jax.experimental import pallas as pl
from jax.experimental.pallas import tpu as pltpu
from jax.sharding import Mesh, PartitionSpec as P

EPSILON = 1e-06
INV_ROOT_TWO = 0.7071067811865476
INV_ROOT_TWO_PI = 0.3989422804014327
F32 = jnp.float32
BF16 = jnp.bfloat16

CHANS = 512
PLANES = 4
HALVES = 2
SUB = PLANES * HALVES
ROWS = 32
COLS = 512
LINE = 128
LINES = 4
SPOTS = LINES * LINE
HID = 256
GROUP = 16
X = 4
Y = 2
PLANE_VMEM = 12 * 1024 * 1024
MLP_VMEM = 56 * 1024 * 1024


def lanes(width=COLS):
    return lax.broadcasted_iota(jnp.int32, (SUB, width), 1)


def sublanes(width=COLS):
    return lax.broadcasted_iota(jnp.int32, (SUB, width), 0)


def turn(value, shift):
    return pltpu.roll(value, shift % value.shape[1], 1)


def pair_lanes(value, step, lane):
    return jnp.where((lane & step) == 0, value + turn(value, -step), turn(value, step) - value)


def loop(count, step, body):
    def some(index, carry):
        for inner in range(step):
            body(index * step + inner)
        return carry

    if count == step:
        some(0, 0)
    else:
        lax.fori_loop(0, count // step, some, 0)


def fill_edges(ref, rows):
    low = sublanes() < PLANES
    for edge in range(2):
        ref[edge] = jnp.where(low, 0.0, pltpu.roll(ref[rows + edge], PLANES, 0))
        ref[rows + 2 + edge] = jnp.where(low, pltpu.roll(ref[2 + edge], PLANES, 0), 0.0)


def convolve(source, rows, step, taps, first, mirrored, target):
    lane = lanes()
    chunk = 4

    def do_chunk(index):
        base = index * chunk
        totals = [None] * chunk
        for move in range(5):
            coefs = []
            for tap_row in range(5):
                place = tap_row * 5 + move
                coefs.append(taps[first + (24 - place if mirrored else place)])
            blocks = [[None] * (COLS // 128) for _ in range(chunk)]
            for block in range(COLS // 128):
                for row in range(chunk + 4):
                    value = source[base + row, :, block * 128 : block * 128 + 128]
                    for out in range(max(0, row - 4), min(chunk, row + 1)):
                        term = coefs[row - out] * value
                        blocks[out][block] = term if blocks[out][block] is None else blocks[out][block] + term
            offset = (move - 2) * step
            for out in range(chunk):
                summed = jnp.concatenate(blocks[out], 1)
                if offset:
                    kept = (lane < COLS - offset) if offset > 0 else (lane >= -offset)
                    summed = jnp.where(kept, turn(summed, -offset), 0.0)
                totals[out] = summed if totals[out] is None else totals[out] + summed
        for out in range(chunk):
            target[base + out] = totals[out]

    loop(rows // chunk, 1, do_chunk)


def wavelet(plane, taps, mirrored, level_1, level_2, level_3, conv_0, conv_1, conv_2, conv_3):
    lane = lanes()
    fill_edges(plane, ROWS)

    def split_1(row):
        upper, lower = plane[2 + 2 * row], plane[3 + 2 * row]
        level_1[0, 2 + row] = pair_lanes(0.5 * (upper + lower), 1, lane)
        level_1[1, 2 + row] = pair_lanes(0.5 * (upper - lower), 1, lane)

    loop(ROWS // 2, 4, split_1)
    fill_edges(level_1.at[0], ROWS // 2)
    fill_edges(level_1.at[1], ROWS // 2)

    for source, target, rows, step in ((level_1.at[0], level_2, ROWS // 4, 2), (level_2, level_3, ROWS // 8, 4)):
        for row in range(rows):
            upper, lower = source[2 + 2 * row], source[3 + 2 * row]
            across = pair_lanes(0.5 * (upper + lower), step, lane)
            down = pair_lanes(0.5 * (upper - lower), step, lane)
            target[2 + row] = jnp.where((lane & (step - 1)) == 0, across, turn(down, 1))
        fill_edges(target, rows)

    convolve(plane, ROWS, 1, taps, 0, mirrored, conv_0)
    convolve(level_1.at[0], ROWS // 2, 2, taps, 25, mirrored, conv_1.at[0])
    convolve(level_1.at[1], ROWS // 2, 2, taps, 50, mirrored, conv_1.at[1])
    convolve(level_2, ROWS // 4, 4, taps, 75, mirrored, conv_2)
    convolve(level_3, ROWS // 8, 8, taps, 100, mirrored, conv_3)

    for source, target, rows, step in ((conv_3, conv_2, ROWS // 8, 4), (conv_2, conv_1.at[0], ROWS // 4, 2)):
        for row in range(rows):
            kept = source[row]
            moved = turn(kept, -1)
            for half, value in ((0, kept + moved), (1, kept - moved)):
                merged = pair_lanes(0.5 * value, step, lane)
                place = 2 * row + half
                target[place] = target[place] + jnp.where((lane & (step - 1)) == 0, merged, 0.0)


def merged_rows(row, conv_1, lane):
    across, down = conv_1[0, row], conv_1[1, row]
    return pair_lanes(0.5 * (across + down), 1, lane), pair_lanes(0.5 * (across - down), 1, lane)


def tile_of(half, row_block, col):
    return (half * 4 + col) * 2 + row_block


def tile_in(tiles, row_block, col):
    parts = [tiles[tile_of(half, row_block, col)].astype(F32) for half in range(HALVES)]
    return jnp.swapaxes(jnp.concatenate(parts, 0), 0, 1)


def regroup(first, second, low):
    return (
        jnp.where(low, first, pltpu.roll(second, PLANES, 0)),
        jnp.where(low, pltpu.roll(first, PLANES, 0), second),
    )


def forward_kernel(tiles, taps, shift, sent, plane, level_1, level_2, level_3, conv_0, conv_1, conv_2, conv_3):
    for row_block in range(2):
        for col in range(4):
            cols = slice(col * LINE, col * LINE + LINE)
            plane[2 + row_block * 16 : 18 + row_block * 16, :, cols] = tile_in(tiles, row_block, col)
    wavelet(plane, taps, False, level_1, level_2, level_3, conv_0, conv_1, conv_2, conv_3)
    lane = lanes()
    bias = shift[...]
    low = sublanes(LINE) < PLANES

    def finish(group):
        rows = []
        for pair in range(LINES // 2):
            merged = merged_rows(2 * group + pair, conv_1, lane)
            for half in range(2):
                rows.append(conv_0[LINES * group + 2 * pair + half] + bias + merged[half])
        for col in range(4):
            cols = slice(col * LINE, col * LINE + LINE)
            pairs = [regroup(rows[q][:, cols], rows[q + 1][:, cols], low) for q in (0, 2)]
            for half in range(HALVES):
                block = jnp.concatenate([pairs[0][half], pairs[1][half]], 0).astype(BF16)
                for twin in range(Y):
                    sent[group % X, twin, tile_of(half, group // X, col)] = block

    loop(ROWS // LINES, 2, finish)


def backward_kernel(
    parts, tiles, taps, scale, shift, sent, plane, level_1, level_2, level_3, conv_0, conv_1, conv_2, conv_3, second
):
    low = sublanes(LINE) < PLANES

    def gather(group):
        for col in range(4):
            cols = slice(col * LINE, col * LINE + LINE)
            both = []
            for half in range(HALVES):
                place = tile_of(half, group // X, col)
                both.append(parts[group % X, 0, place].astype(F32) + parts[group % X, 1, place].astype(F32))
            for start, target, first in ((0, second, 0), (2 * SUB, plane, 2)):
                for pair in range(LINES // 2):
                    area = slice(start + pair * SUB, start + pair * SUB + SUB)
                    rows = regroup(both[0][area], both[1][area], low)
                    for half in range(2):
                        target[first + LINES * group + 2 * pair + half, :, cols] = rows[half]

    loop(ROWS // LINES, 2, gather)
    wavelet(plane, taps, True, level_1, level_2, level_3, conv_0, conv_1, conv_2, conv_3)
    lane = lanes()

    def finish(pair):
        rows = merged_rows(pair, conv_1, lane)
        for half in range(2):
            row = 2 * pair + half
            conv_0[row] = conv_0[row] + rows[half]

    loop(ROWS // 2, 4, finish)
    layer, bias = scale[...], shift[...]
    for row_block in range(2):
        for col in range(4):
            cols = slice(col * LINE, col * LINE + LINE)
            rows = slice(row_block * 16, row_block * 16 + 16)
            projected = layer[:, cols] * (second[rows, :, cols] + bias[:, cols])
            output = tile_in(tiles, row_block, col) + projected
            for first, value in ((0, output), (PLANES, conv_0[rows, :, cols])):
                turned = jnp.swapaxes(value, 0, 1).astype(BF16)
                for half in range(HALVES):
                    place = tile_of(half, row_block, col)
                    sent[place, first : first + PLANES] = turned[half * PLANES : half * PLANES + PLANES]


def plane_scratch():
    return [
        pltpu.VMEM((ROWS + 4, SUB, COLS), F32),
        pltpu.VMEM((2, ROWS // 2 + 4, SUB, COLS), F32),
        pltpu.VMEM((ROWS // 4 + 4, SUB, COLS), F32),
        pltpu.VMEM((ROWS // 8 + 4, SUB, COLS), F32),
        pltpu.VMEM((ROWS, SUB, COLS), F32),
        pltpu.VMEM((2, ROWS // 2, SUB, COLS), F32),
        pltpu.VMEM((ROWS // 4, SUB, COLS), F32),
        pltpu.VMEM((ROWS // 8, SUB, COLS), F32),
    ]


def dot(left, right, left_dim, right_dim):
    return lax.dot_general(left, right, (((left_dim,), (right_dim,)), ((), ())), preferred_element_type=F32)


def hidden_parts(pack, core, bias, normed_turned, scaled_turned):
    mine, others = pack[0, :CHANS], pack[1, :CHANS]
    w_in = jnp.where(core == 0, mine, others)
    w_out = jnp.where(core == 0, others, mine)
    w_out = jnp.concatenate([w_out[:HID], w_out[HID:]], 1).T
    hidden = dot(normed_turned, w_in, 1, 0) + bias
    spread = 0.5 * (1.0 + lax.erf(hidden * INV_ROOT_TWO))
    activated = (hidden * spread).astype(BF16)
    slope = spread + hidden * jnp.exp(-0.5 * hidden * hidden) * INV_ROOT_TWO_PI
    grad_hidden = (dot(scaled_turned, w_out, 1, 0) * slope).astype(BF16)
    return w_in, w_out, activated, grad_hidden


def mlp_kernel(
    order, biases, gain, bias, received_at, received_scaled_at,
    mine_0, mine_1, mine_2, mine_3, others_0, others_1, others_2, others_3, sent_at, kept_at, given_at,
    received, received_scaled, packs, mixed, scaled, projected, grads, sent, kept, given, arrived, left,
):
    halves = ((mine_0, others_0), (mine_1, others_1), (mine_2, others_2), (mine_3, others_3))
    sources = (received_at, received_scaled_at, *[half for pair in halves for half in pair])
    targets = (received, received_scaled, *[packs.at[index, half] for index in range(X) for half in range(2)])
    arrivals = [
        pltpu.make_async_copy(source, target, arrived.at[i]) for i, (source, target) in enumerate(zip(sources, targets))
    ]
    for copy in arrivals:
        copy.start()
    departures = []

    def depart(source, target):
        copy = pltpu.make_async_copy(source, target, left.at[len(departures)])
        copy.start()
        departures.append(copy)

    arrivals[0].wait()
    low = sublanes(LINE) < PLANES

    def arrange(index):
        for pair in range(2):
            one = received[4 * index + 2 * pair].astype(F32)
            two = received[4 * index + 2 * pair + 1].astype(F32)
            rows = pl.ds(pl.multiple_of(index * 16 + pair * SUB, SUB), SUB)
            for half in range(2):
                area = slice(half * SUB, half * SUB + SUB)
                lines = regroup(one[area], two[area], low)
                for line in range(2):
                    place = (2 * half + line) * LINE
                    mixed[rows, place : place + LINE] = lines[line]

    loop(CHANS // 16, 4, arrange)
    arrivals[1].wait()
    share = CHANS // (X * Y)
    for block in range(X * Y):
        for line in range(LINES):
            scaled[block * share : block * share + share, line * LINE : line * LINE + LINE] = received_scaled[block, line]
    values = mixed[...]
    average = jnp.sum(values, 0, keepdims=True) / CHANS
    rescale = lax.rsqrt(jnp.sum(values * values, 0, keepdims=True) / CHANS - average * average + EPSILON)
    gains = gain[...]
    normed = (((values - average) * rescale) * gains + bias[...]).astype(BF16)
    scaled_now = scaled[...]
    normed_turned, scaled_turned = normed.T, scaled_now.T
    for index in range(X):
        arrivals[2 + 2 * index].wait()
        arrivals[3 + 2 * index].wait()
        w_in, w_out, activated, grad_hidden = hidden_parts(
            packs.at[index], order[1], biases[index : index + 1], normed_turned, scaled_turned
        )
        part = dot(w_out, activated, 1, 1)
        projected[...] = part if index == 0 else projected[...] + part
        part = dot(w_in, grad_hidden, 1, 1)
        grads[...] = part if index == 0 else grads[...] + part
        owner = order[0] ^ index
        for arr, value in ((0, dot(normed, grad_hidden, 1, 0)), (1, dot(scaled_now, activated, 1, 0))):
            rounded = value.astype(BF16)
            for piece in range(GROUP // 2):
                first, second = rounded[piece * 64 : piece * 64 + 32], rounded[piece * 64 + 32 : piece * 64 + 64]
                for part in range(4):
                    cut = (slice(part % 2 * 16, part % 2 * 16 + 16), slice(part // 2 * 128, part // 2 * 128 + 128))
                    kept[owner, piece, arr * 4 + part] = jnp.where(order[1] == 0, first[cut], second[cut])
                    given[owner, piece, arr * 4 + part] = jnp.where(order[1] == 0, second[cut], first[cut])
        depart(given.at[owner], given_at.at[owner])
        depart(kept.at[owner], kept_at.at[owner])
    weighted = grads[...] * gains
    centred = (mixed[...] - average) * rescale
    sum_one = jnp.sum(weighted, 0, keepdims=True) / CHANS
    sum_two = jnp.sum(weighted * centred, 0, keepdims=True) / CHANS
    grads[...] = rescale * (weighted - sum_one - centred * sum_two)

    def hand_out(index):
        rows = pl.ds(pl.multiple_of(index * SUB, SUB), SUB)
        blocks = [[], []]
        for ref in (projected, grads):
            value = ref[rows]
            for half in range(2):
                place = 2 * half * LINE
                pair = regroup(value[:, place : place + LINE], value[:, place + LINE : place + 2 * LINE], low)
                for which in range(2):
                    blocks[which].append(pair[which])
        for which in range(2):
            sent[2 * index + which] = jnp.concatenate(blocks[which], 0).astype(BF16)

    quarter = CHANS // SUB // 4
    for part in range(4):
        loop(quarter, 4, lambda index: hand_out(part * quarter + index))
        area = pl.ds(part * 2 * quarter, 2 * quarter)
        depart(sent.at[area], sent_at.at[area])
    for copy in departures:
        copy.wait()


def finish_kernel(results, cotangent, output_map, grad_map, grad_in, grad_out):
    output_map[...] = results[:, :PLANES]
    grad_map[...] = (cotangent[...].astype(F32) + results[:, PLANES : 2 * PLANES].astype(F32)).astype(BF16)
    factor = 1.0 / (64.0 * 512.0) ** 0.5
    for half in range(2):
        cols = slice(half * 128, half * 128 + 128)
        for pair in range(GROUP // 4):
            blocks = []
            for piece in range(4 * pair, 4 * pair + 4):
                for part in range(2):
                    rows = slice(piece * 32 + part * 16, piece * 32 + part * 16 + 16)
                    grad_in[rows, cols] = results[piece, 2 * PLANES + half * 2 + part].astype(F32) * factor
                    blocks.append(results[piece, 2 * PLANES + 4 + half * 2 + part])
            block = jnp.concatenate(blocks, 0).astype(F32) * factor
            grad_out[cols, pair * 128 : pair * 128 + 128] = block.T


def call(kernel, outs, scratch, ops):
    spaces = [
        pl.BlockSpec(memory_space=pltpu.SMEM if op.dtype == jnp.int32 else pltpu.VMEM) for op in ops
    ]
    out_spaces = jax.tree.map(lambda _: pl.BlockSpec(memory_space=pltpu.VMEM), outs)
    return pl.pallas_call(
        kernel,
        out_shape=outs,
        in_specs=spaces,
        out_specs=out_spaces,
        scratch_shapes=scratch,
        compiler_params=pltpu.CompilerParams(vmem_limit_bytes=PLANE_VMEM),
    )(*ops)


def prepare_kernel(order, cotangent, layer, w_in, w_out, b_in, norms, other, scaled, mine, others):
    for block in range(0, CHANS // (X * Y), 16):
        rows = [
            jnp.swapaxes(cotangent[part : part + SUB].astype(F32) * layer[part : part + SUB], 0, 1)
            for part in (block, block + SUB)
        ]
        rounded = jnp.concatenate(rows, 1).astype(BF16)
        for where in range(X):
            for twin in range(Y):
                scaled[where * Y + twin, :, block : block + 16] = rounded[where * LINES : where * LINES + LINES]
    for half in range(2):
        area = slice(half * HID, half * HID + HID)
        first, second = w_in[area], w_out[:, area]
        mine[area] = jnp.where(order[1] == 0, first, second)
        others[area] = jnp.where(order[1] == 0, second, first)
    left = [b_in[...], jnp.concatenate([norms[...], other[...]], 1)]
    rows = []
    for _ in range(3):
        parts = [value.astype(BF16).astype(F32) for value in left]
        left = [value - part for value, part in zip(left, parts)]
        rows.extend(parts)
    small = jnp.concatenate(rows + [jnp.zeros((10, HID), F32)], 0).astype(BF16)
    mine[CHANS:] = small
    others[CHANS:] = small


def summed(*terms):
    total = terms[0].astype(F32)
    for term in terms[1:]:
        total = total + term.astype(F32)
    return total.astype(BF16)


def own_planes(array, dim, place):
    return lax.dynamic_slice_in_dim(array, place * PLANES, PLANES, dim)


def over_halves(array):
    return jnp.concatenate([array, array], -2)


def tap_table(base_kernel, base_scale, wave_kernels, wave_scale):
    base = (base_scale[:, None, None] * base_kernel).reshape(PLANES, 25).T[:, :, None]
    waves = (wave_scale[..., None, None] * wave_kernels).reshape(3, PLANES, 4, 25).transpose(0, 2, 3, 1)[..., None]
    lane = jnp.arange(128)[None, None, :]

    def choose(level, period, bands):
        table = jnp.zeros((25, PLANES, 128), F32)
        for residue, band in bands:
            table = jnp.where(lane % period == residue, waves[level, band], table)
        return table

    tables = [
        jnp.broadcast_to(base, (25, PLANES, 128)),
        choose(0, 2, ((0, 0), (1, 1))),
        choose(0, 2, ((0, 2), (1, 3))),
        choose(1, 4, ((0, 0), (2, 1), (1, 2), (3, 3))),
        choose(2, 8, ((0, 0), (4, 1), (1, 2), (5, 3))),
    ]
    return over_halves(jnp.concatenate(tables, 0))


def on_device(
    feature_map,
    base_kernel,
    base_bias,
    base_scale,
    wave_kernels,
    wave_scale,
    norm_gain,
    norm_bias,
    w_in,
    b_in,
    w_out,
    b_out,
    layer_scale,
    cotangent,
):
    group = ("hi", "col", "core")
    everyone = ("x", "y", "hi", "col", "core")
    core_here = lax.axis_index("core")
    place = lax.axis_index("hi") * 8 + lax.axis_index("col") * 2 + core_here
    x_here = lax.axis_index("x")
    y_here = lax.axis_index("y")

    tiles = lax.all_to_all(
        feature_map.reshape(GROUP, PLANES, 16, 128), group, split_axis=0, concat_axis=0, tiled=True
    )
    share = CHANS // (X * Y)
    norms = jnp.concatenate([norm_gain, norm_bias]).reshape(1, 2 * share)
    other = lax.ppermute(norms, "y", [(0, 1), (1, 0)])
    order = jnp.stack([x_here, core_here]).astype(jnp.int32)
    scaled, mine, others = call(
        prepare_kernel,
        (
            jax.ShapeDtypeStruct((X * Y, LINES, share, LINE), BF16),
            jax.ShapeDtypeStruct((CHANS + 16, HID), BF16),
            jax.ShapeDtypeStruct((CHANS + 16, HID), BF16),
        ),
        [],
        (
            order,
            cotangent,
            jnp.broadcast_to(layer_scale[:, None, None], (share, 1, LINE)),
            w_in,
            w_out,
            b_in.reshape(1, HID),
            norms,
            other,
        ),
    )
    mine = [mine] + [lax.ppermute(mine, "x", [(i, i ^ step) for i in range(X)]) for step in range(1, X)]
    others = [others] + [lax.ppermute(one, "core", [(0, 1), (1, 0)]) for one in mine[1:]]
    scaled = lax.all_to_all(scaled, ("x", "y"), split_axis=0, concat_axis=0, tiled=True)

    scale_own = own_planes(base_scale, 0, place)
    taps = tap_table(
        own_planes(base_kernel, 0, place),
        scale_own,
        own_planes(wave_kernels, 1, place),
        own_planes(wave_scale, 1, place),
    )

    def rows_of(vector):
        return over_halves(jnp.broadcast_to(vector[:, None], (PLANES, COLS)))

    layer = rows_of(own_planes(layer_scale, 0, place))
    sent = call(
        forward_kernel,
        jax.ShapeDtypeStruct((X, Y, GROUP, 2 * SUB, LINE), BF16),
        plane_scratch(),
        (tiles, taps, rows_of(scale_own * own_planes(base_bias, 0, place))),
    )
    received = lax.all_to_all(
        sent.reshape(X * Y * GROUP, 2 * SUB, LINE), everyone, split_axis=0, concat_axis=0, tiled=True
    )

    extras = jnp.stack([one[CHANS : CHANS + 6] for one in mine])
    extras = jnp.sum(extras.reshape(X, 3, 2, HID).astype(F32), 1)
    biases = extras[:, 0]
    norms = extras[:, 1].reshape(X, Y, 2, share)[x_here ^ jnp.arange(X)][:, y_here ^ jnp.arange(Y)]
    vectors = norms.transpose(2, 0, 1, 3).reshape(2, CHANS, 1)

    anywhere = pl.BlockSpec(memory_space=pl.ANY)
    nearby = pl.BlockSpec(memory_space=pltpu.VMEM)
    blocks = (X * Y * GROUP, 4 * SUB, LINE)
    pieces = (X, GROUP // 2, 8, 16, 128)
    sent, kept, given = pl.pallas_call(
        mlp_kernel,
        out_shape=tuple(jax.ShapeDtypeStruct(shape, BF16) for shape in (blocks, pieces, pieces)),
        in_specs=[pl.BlockSpec(memory_space=pltpu.SMEM)] + [nearby] * 3 + [anywhere] * 10,
        out_specs=(anywhere,) * 3,
        scratch_shapes=[
            pltpu.VMEM(received.shape, BF16),
            pltpu.VMEM(scaled.shape, BF16),
            pltpu.VMEM((X, 2, CHANS + 16, HID), BF16),
            pltpu.VMEM((CHANS, SPOTS), F32),
            pltpu.VMEM((CHANS, SPOTS), BF16),
            pltpu.VMEM((CHANS, SPOTS), F32),
            pltpu.VMEM((CHANS, SPOTS), F32),
            pltpu.VMEM(blocks, BF16),
            pltpu.VMEM(pieces, BF16),
            pltpu.VMEM(pieces, BF16),
            pltpu.SemaphoreType.DMA((10,)),
            pltpu.SemaphoreType.DMA((12,)),
        ],
        compiler_params=pltpu.CompilerParams(vmem_limit_bytes=MLP_VMEM),
    )(
        order,
        biases,
        vectors[0],
        vectors[1],
        received,
        scaled,
        *mine,
        *others,
    )
    received = lax.all_to_all(sent, everyone, split_axis=0, concat_axis=0, tiled=True)

    given = lax.ppermute(given, "core", [(0, 1), (1, 0)])
    pieces = summed(kept, given).reshape(X * GROUP // 2, 8, 16, 128)
    pieces = lax.all_to_all(pieces, ("x", "hi", "col"), split_axis=0, concat_axis=0, tiled=True)
    piece = jnp.sum(pieces.astype(F32), 0).astype(BF16)

    sent = call(
        backward_kernel,
        jax.ShapeDtypeStruct((GROUP, 2 * PLANES, 16, 128), BF16),
        plane_scratch() + [pltpu.VMEM((ROWS, SUB, COLS), F32)],
        (
            received.reshape(X, Y, GROUP, 4 * SUB, LINE),
            tiles,
            taps,
            layer,
            rows_of(own_planes(b_out, 0, place)),
        ),
    )
    sent = jnp.concatenate([sent, jnp.broadcast_to(piece, (GROUP,) + piece.shape)], 1)
    results = lax.all_to_all(sent, group, split_axis=0, concat_axis=0, tiled=True)
    output_map, grad_map, grad_in, grad_out = call(
        finish_kernel,
        (
            jax.ShapeDtypeStruct((GROUP, PLANES, 16, 128), BF16),
            jax.ShapeDtypeStruct((GROUP, PLANES, 16, 128), BF16),
            jax.ShapeDtypeStruct((CHANS, HID), F32),
            jax.ShapeDtypeStruct((HID, CHANS), F32),
        ),
        [],
        (results, cotangent.reshape(GROUP, PLANES, 16, 128)),
    )
    output_map, grad_map = output_map.reshape(feature_map.shape), grad_map.reshape(feature_map.shape)
    return (output_map, grad_map, grad_in, grad_out)


def solution(mesh):
    grid = Mesh(mesh.devices.reshape(2, 2, 4, X, Y), ("hi", "core", "col", "x", "y"))
    chan, row = ("x", "y"), ("hi", "core")
    return jax.shard_map(
        on_device,
        mesh=grid,
        in_specs=(
            P(chan, row, "col"),
            P(chan, None, None),
            P(chan),
            P(chan),
            P(None, chan, None, None, None),
            P(None, chan, None),
            P(chan),
            P(chan),
            P(None, chan),
            P(chan),
            P(chan, None),
            P(chan),
            P(chan),
            P(chan, row, "col"),
        ),
        out_specs=(
            P(chan, row, "col"),
            P(chan, row, "col"),
            P(None, chan),
            P(chan, None),
        ),
        check_vma=False,
    )
```

```python
import jax
import jax.numpy as jnp
from jax import lax
from jax.experimental import pallas as pl
from jax.experimental.pallas import tpu as pltpu
from jax.sharding import Mesh, PartitionSpec as P

EPSILON = 1e-06
INV_ROOT_TWO = 0.7071067811865476
INV_ROOT_TWO_PI = 0.3989422804014327
F32 = jnp.float32
BF16 = jnp.bfloat16

CHANS = 512
PLANES = 4
HALVES = 2
SUB = PLANES * HALVES
ROWS = 32
COLS = 512
LINE = 128
LINES = 4
SPOTS = LINES * LINE
HID = 256
GROUP = 16
X = 4
Y = 2
PLANE_VMEM = 12 * 1024 * 1024
MLP_VMEM = 56 * 1024 * 1024


def lanes(width=COLS):
    return lax.broadcasted_iota(jnp.int32, (SUB, width), 1)


def sublanes(width=COLS):
    return lax.broadcasted_iota(jnp.int32, (SUB, width), 0)


def turn(value, shift):
    return pltpu.roll(value, shift % value.shape[1], 1)


def pair_lanes(value, step, lane):
    return jnp.where((lane & step) == 0, value + turn(value, -step), turn(value, step) - value)


def loop(count, step, body):
    def some(index, carry):
        for inner in range(step):
            body(index * step + inner)
        return carry

    if count == step:
        some(0, 0)
    else:
        lax.fori_loop(0, count // step, some, 0)


def fill_edges(ref, rows):
    low = sublanes() < PLANES
    for edge in range(2):
        ref[edge] = jnp.where(low, 0.0, pltpu.roll(ref[rows + edge], PLANES, 0))
        ref[rows + 2 + edge] = jnp.where(low, pltpu.roll(ref[2 + edge], PLANES, 0), 0.0)


def convolve(source, rows, step, taps, first, mirrored, target):
    lane = lanes()
    chunk = 4

    def do_chunk(index):
        base = index * chunk
        totals = [None] * chunk
        for move in range(5):
            coefs = []
            for tap_row in range(5):
                place = tap_row * 5 + move
                coefs.append(taps[first + (24 - place if mirrored else place)])
            blocks = [[None] * (COLS // 128) for _ in range(chunk)]
            for block in range(COLS // 128):
                for row in range(chunk + 4):
                    value = source[base + row, :, block * 128 : block * 128 + 128]
                    for out in range(max(0, row - 4), min(chunk, row + 1)):
                        term = coefs[row - out] * value
                        blocks[out][block] = term if blocks[out][block] is None else blocks[out][block] + term
            offset = (move - 2) * step
            for out in range(chunk):
                summed = jnp.concatenate(blocks[out], 1)
                if offset:
                    kept = (lane < COLS - offset) if offset > 0 else (lane >= -offset)
                    summed = jnp.where(kept, turn(summed, -offset), 0.0)
                totals[out] = summed if totals[out] is None else totals[out] + summed
        for out in range(chunk):
            target[base + out] = totals[out]

    loop(rows // chunk, 1, do_chunk)


def wavelet(plane, taps, mirrored, level_1, level_2, level_3, conv_0, conv_1, conv_2, conv_3):
    lane = lanes()
    fill_edges(plane, ROWS)

    def split_1(row):
        upper, lower = plane[2 + 2 * row], plane[3 + 2 * row]
        level_1[0, 2 + row] = pair_lanes(0.5 * (upper + lower), 1, lane)
        level_1[1, 2 + row] = pair_lanes(0.5 * (upper - lower), 1, lane)

    loop(ROWS // 2, 4, split_1)
    fill_edges(level_1.at[0], ROWS // 2)
    fill_edges(level_1.at[1], ROWS // 2)

    for source, target, rows, step in ((level_1.at[0], level_2, ROWS // 4, 2), (level_2, level_3, ROWS // 8, 4)):
        for row in range(rows):
            upper, lower = source[2 + 2 * row], source[3 + 2 * row]
            across = pair_lanes(0.5 * (upper + lower), step, lane)
            down = pair_lanes(0.5 * (upper - lower), step, lane)
            target[2 + row] = jnp.where((lane & (step - 1)) == 0, across, turn(down, 1))
        fill_edges(target, rows)

    convolve(plane, ROWS, 1, taps, 0, mirrored, conv_0)
    convolve(level_1.at[0], ROWS // 2, 2, taps, 25, mirrored, conv_1.at[0])
    convolve(level_1.at[1], ROWS // 2, 2, taps, 50, mirrored, conv_1.at[1])
    convolve(level_2, ROWS // 4, 4, taps, 75, mirrored, conv_2)
    convolve(level_3, ROWS // 8, 8, taps, 100, mirrored, conv_3)

    for source, target, rows, step in ((conv_3, conv_2, ROWS // 8, 4), (conv_2, conv_1.at[0], ROWS // 4, 2)):
        for row in range(rows):
            kept = source[row]
            moved = turn(kept, -1)
            for half, value in ((0, kept + moved), (1, kept - moved)):
                merged = pair_lanes(0.5 * value, step, lane)
                place = 2 * row + half
                target[place] = target[place] + jnp.where((lane & (step - 1)) == 0, merged, 0.0)


def merged_rows(row, conv_1, lane):
    across, down = conv_1[0, row], conv_1[1, row]
    return pair_lanes(0.5 * (across + down), 1, lane), pair_lanes(0.5 * (across - down), 1, lane)


def tile_of(half, row_block, col):
    return (half * 4 + col) * 2 + row_block


def tile_in(tiles, row_block, col):
    parts = [tiles[tile_of(half, row_block, col)].astype(F32) for half in range(HALVES)]
    return jnp.swapaxes(jnp.concatenate(parts, 0), 0, 1)


def regroup(first, second, low):
    return (
        jnp.where(low, first, pltpu.roll(second, PLANES, 0)),
        jnp.where(low, pltpu.roll(first, PLANES, 0), second),
    )


def forward_kernel(tiles, taps, shift, sent, plane, level_1, level_2, level_3, conv_0, conv_1, conv_2, conv_3):
    for row_block in range(2):
        for col in range(4):
            cols = slice(col * LINE, col * LINE + LINE)
            plane[2 + row_block * 16 : 18 + row_block * 16, :, cols] = tile_in(tiles, row_block, col)
    wavelet(plane, taps, False, level_1, level_2, level_3, conv_0, conv_1, conv_2, conv_3)
    lane = lanes()
    bias = shift[...]
    low = sublanes(LINE) < PLANES

    def finish(group):
        rows = []
        for pair in range(LINES // 2):
            merged = merged_rows(2 * group + pair, conv_1, lane)
            for half in range(2):
                rows.append(conv_0[LINES * group + 2 * pair + half] + bias + merged[half])
        for col in range(4):
            cols = slice(col * LINE, col * LINE + LINE)
            pairs = [regroup(rows[q][:, cols], rows[q + 1][:, cols], low) for q in (0, 2)]
            for half in range(HALVES):
                block = jnp.concatenate([pairs[0][half], pairs[1][half]], 0).astype(BF16)
                for twin in range(Y):
                    sent[group % X, twin, tile_of(half, group // X, col)] = block

    loop(ROWS // LINES, 2, finish)


def backward_kernel(
    parts, tiles, taps, scale, shift, sent, plane, level_1, level_2, level_3, conv_0, conv_1, conv_2, conv_3, second
):
    low = sublanes(LINE) < PLANES

    def gather(group):
        for col in range(4):
            cols = slice(col * LINE, col * LINE + LINE)
            both = []
            for half in range(HALVES):
                place = tile_of(half, group // X, col)
                both.append(parts[group % X, 0, place].astype(F32) + parts[group % X, 1, place].astype(F32))
            for start, target, first in ((0, second, 0), (2 * SUB, plane, 2)):
                for pair in range(LINES // 2):
                    area = slice(start + pair * SUB, start + pair * SUB + SUB)
                    rows = regroup(both[0][area], both[1][area], low)
                    for half in range(2):
                        target[first + LINES * group + 2 * pair + half, :, cols] = rows[half]

    loop(ROWS // LINES, 2, gather)
    wavelet(plane, taps, True, level_1, level_2, level_3, conv_0, conv_1, conv_2, conv_3)
    lane = lanes()

    def finish(pair):
        rows = merged_rows(pair, conv_1, lane)
        for half in range(2):
            row = 2 * pair + half
            conv_0[row] = conv_0[row] + rows[half]

    loop(ROWS // 2, 4, finish)
    layer, bias = scale[...], shift[...]
    for row_block in range(2):
        for col in range(4):
            cols = slice(col * LINE, col * LINE + LINE)
            rows = slice(row_block * 16, row_block * 16 + 16)
            projected = layer[:, cols] * (second[rows, :, cols] + bias[:, cols])
            output = tile_in(tiles, row_block, col) + projected
            for first, value in ((0, output), (PLANES, conv_0[rows, :, cols])):
                turned = jnp.swapaxes(value, 0, 1).astype(BF16)
                for half in range(HALVES):
                    place = tile_of(half, row_block, col)
                    sent[place, first : first + PLANES] = turned[half * PLANES : half * PLANES + PLANES]


def plane_scratch():
    return [
        pltpu.VMEM((ROWS + 4, SUB, COLS), F32),
        pltpu.VMEM((2, ROWS // 2 + 4, SUB, COLS), F32),
        pltpu.VMEM((ROWS // 4 + 4, SUB, COLS), F32),
        pltpu.VMEM((ROWS // 8 + 4, SUB, COLS), F32),
        pltpu.VMEM((ROWS, SUB, COLS), F32),
        pltpu.VMEM((2, ROWS // 2, SUB, COLS), F32),
        pltpu.VMEM((ROWS // 4, SUB, COLS), F32),
        pltpu.VMEM((ROWS // 8, SUB, COLS), F32),
    ]


def dot(left, right, left_dim, right_dim):
    return lax.dot_general(left, right, (((left_dim,), (right_dim,)), ((), ())), preferred_element_type=F32)


def hidden_parts(pack, core, bias, normed_turned, scaled_turned):
    mine, others = pack[0, :CHANS], pack[1, :CHANS]
    w_in = jnp.where(core == 0, mine, others)
    w_out = jnp.where(core == 0, others, mine)
    w_out = jnp.concatenate([w_out[:HID], w_out[HID:]], 1).T
    hidden = dot(normed_turned, w_in, 1, 0) + bias
    spread = 0.5 * (1.0 + lax.erf(hidden * INV_ROOT_TWO))
    activated = (hidden * spread).astype(BF16)
    slope = spread + hidden * jnp.exp(-0.5 * hidden * hidden) * INV_ROOT_TWO_PI
    grad_hidden = (dot(scaled_turned, w_out, 1, 0) * slope).astype(BF16)
    return w_in, w_out, activated, grad_hidden


def mlp_kernel(
    order, biases, vectors, received_at, received_scaled_at,
    mine_0, mine_1, mine_2, mine_3, others_0, others_1, others_2, others_3, sent_at, kept_at, given_at,
    received, received_scaled, packs, mixed, scaled, projected, grads, sent, kept, given, arrived, left,
):
    halves = ((mine_0, others_0), (mine_1, others_1), (mine_2, others_2), (mine_3, others_3))
    sources = (received_at, received_scaled_at, *[half for pair in halves for half in pair])
    targets = (received, received_scaled, *[packs.at[index, half] for index in range(X) for half in range(2)])
    arrivals = [
        pltpu.make_async_copy(source, target, arrived.at[i]) for i, (source, target) in enumerate(zip(sources, targets))
    ]
    for copy in arrivals:
        copy.start()
    departures = []

    def depart(source, target):
        copy = pltpu.make_async_copy(source, target, left.at[len(departures)])
        copy.start()
        departures.append(copy)

    arrivals[0].wait()
    low = sublanes(LINE) < PLANES

    def arrange(index):
        for pair in range(2):
            one = received[4 * index + 2 * pair].astype(F32)
            two = received[4 * index + 2 * pair + 1].astype(F32)
            rows = pl.ds(pl.multiple_of(index * 16 + pair * SUB, SUB), SUB)
            for half in range(2):
                area = slice(half * SUB, half * SUB + SUB)
                lines = regroup(one[area], two[area], low)
                for line in range(2):
                    place = (2 * half + line) * LINE
                    mixed[rows, place : place + LINE] = lines[line]

    loop(CHANS // 16, 4, arrange)
    arrivals[1].wait()
    share = CHANS // (X * Y)
    for block in range(X * Y):
        for line in range(LINES):
            scaled[block * share : block * share + share, line * LINE : line * LINE + LINE] = received_scaled[block, line]
    values = mixed[...]
    average = jnp.sum(values, 0, keepdims=True) / CHANS
    rescale = lax.rsqrt(jnp.sum(values * values, 0, keepdims=True) / CHANS - average * average + EPSILON)
    gains, shifts = [
        jnp.concatenate([jnp.broadcast_to(vectors[row : row + 1], (LINE, CHANS)).T] * (SPOTS // LINE), 1)
        for row in range(2)
    ]
    normed = (((values - average) * rescale) * gains + shifts).astype(BF16)
    scaled_now = scaled[...]
    normed_turned, scaled_turned = normed.T, scaled_now.T
    for index in range(X):
        arrivals[2 + 2 * index].wait()
        arrivals[3 + 2 * index].wait()
        w_in, w_out, activated, grad_hidden = hidden_parts(
            packs.at[index], order[1], biases[index : index + 1], normed_turned, scaled_turned
        )
        part = dot(w_out, activated, 1, 1)
        projected[...] = part if index == 0 else projected[...] + part
        part = dot(w_in, grad_hidden, 1, 1)
        grads[...] = part if index == 0 else grads[...] + part
        for arr, value in ((0, dot(normed, grad_hidden, 1, 0)), (1, dot(scaled_now, activated, 1, 0))):
            rounded = value.astype(BF16)
            for piece in range(GROUP // 2):
                first, second = rounded[piece * 64 : piece * 64 + 32], rounded[piece * 64 + 32 : piece * 64 + 64]
                for part in range(4):
                    cut = (slice(part % 2 * 16, part % 2 * 16 + 16), slice(part // 2 * 128, part // 2 * 128 + 128))
                    kept[index, piece, arr * 4 + part] = jnp.where(order[1] == 0, first[cut], second[cut])
                    given[index, piece, arr * 4 + part] = jnp.where(order[1] == 0, second[cut], first[cut])
        depart(given.at[index], given_at.at[index])
        depart(kept.at[index], kept_at.at[index])
    weighted = grads[...] * gains
    centred = (mixed[...] - average) * rescale
    sum_one = jnp.sum(weighted, 0, keepdims=True) / CHANS
    sum_two = jnp.sum(weighted * centred, 0, keepdims=True) / CHANS
    grads[...] = rescale * (weighted - sum_one - centred * sum_two)

    def hand_out(index):
        rows = pl.ds(pl.multiple_of(index * SUB, SUB), SUB)
        blocks = [[], []]
        for ref in (projected, grads):
            value = ref[rows]
            for half in range(2):
                place = 2 * half * LINE
                pair = regroup(value[:, place : place + LINE], value[:, place + LINE : place + 2 * LINE], low)
                for which in range(2):
                    blocks[which].append(pair[which])
        for which in range(2):
            sent[2 * index + which] = jnp.concatenate(blocks[which], 0).astype(BF16)

    quarter = CHANS // SUB // 4
    for part in range(4):
        loop(quarter, 4, lambda index: hand_out(part * quarter + index))
        area = pl.ds(part * 2 * quarter, 2 * quarter)
        depart(sent.at[area], sent_at.at[area])
    for copy in departures:
        copy.wait()


def sum_kernel(first, second, third, fourth, after, total):
    for place in range(first.shape[0]):
        parts = [ref[place].astype(F32) for ref in (first, second, third, fourth)]
        total[place] = (parts[0] + parts[1] + parts[2] + parts[3]).astype(BF16)


def finish_kernel(results, cotangent, output_map, grad_map, grad_in, grad_out):
    output_map[...] = results[:, :PLANES]
    grad_map[...] = (cotangent[...].astype(F32) + results[:, PLANES : 2 * PLANES].astype(F32)).astype(BF16)
    factor = 1.0 / (64.0 * 512.0) ** 0.5
    for half in range(2):
        cols = slice(half * 128, half * 128 + 128)
        for pair in range(GROUP // 4):
            blocks = []
            for piece in range(4 * pair, 4 * pair + 4):
                for part in range(2):
                    rows = slice(piece * 32 + part * 16, piece * 32 + part * 16 + 16)
                    grad_in[rows, cols] = results[piece, 2 * PLANES + half * 2 + part].astype(F32) * factor
                    blocks.append(results[piece, 2 * PLANES + 4 + half * 2 + part])
            block = jnp.concatenate(blocks, 0).astype(F32) * factor
            grad_out[cols, pair * 128 : pair * 128 + 128] = block.T


def call(kernel, outs, scratch, ops, microseconds):
    spaces = [
        pl.BlockSpec(memory_space=pltpu.SMEM if op.dtype == jnp.int32 else pltpu.VMEM) for op in ops
    ]
    out_spaces = jax.tree.map(lambda _: pl.BlockSpec(memory_space=pltpu.VMEM), outs)
    return pl.pallas_call(
        kernel,
        out_shape=outs,
        in_specs=spaces,
        out_specs=out_spaces,
        scratch_shapes=scratch,
        compiler_params=pltpu.CompilerParams(vmem_limit_bytes=PLANE_VMEM),
        cost_estimate=pl.CostEstimate(flops=0, bytes_accessed=int(microseconds * 3.5e6), transcendentals=0),
    )(*ops)


def prepare_kernel(order, cotangent, layer, w_in, w_out, b_in, norms, other, scaled, mine, others):
    for block in range(0, CHANS // (X * Y), 16):
        rows = [
            jnp.swapaxes(cotangent[part : part + SUB].astype(F32) * layer[part : part + SUB], 0, 1)
            for part in (block, block + SUB)
        ]
        rounded = jnp.concatenate(rows, 1).astype(BF16)
        for where in range(X):
            for twin in range(Y):
                scaled[where * Y + twin, :, block : block + 16] = rounded[where * LINES : where * LINES + LINES]
    for half in range(2):
        area = slice(half * HID, half * HID + HID)
        first, second = w_in[area], w_out[:, area]
        mine[area] = jnp.where(order[1] == 0, first, second)
        others[area] = jnp.where(order[1] == 0, second, first)
    left = [b_in[...], jnp.concatenate([norms[...], other[...]], 1)]
    rows = []
    for _ in range(3):
        parts = [value.astype(BF16).astype(F32) for value in left]
        left = [value - part for value, part in zip(left, parts)]
        rows.extend(parts)
    small = jnp.concatenate(rows + [jnp.zeros((10, HID), F32)], 0).astype(BF16)
    mine[CHANS:] = small
    others[CHANS:] = small


def summed(*terms):
    total = terms[0].astype(F32)
    for term in terms[1:]:
        total = total + term.astype(F32)
    return total.astype(BF16)


def own_planes(array, dim, place):
    return lax.dynamic_slice_in_dim(array, place * PLANES, PLANES, dim)


def over_halves(array):
    return jnp.concatenate([array, array], -2)


def tap_table(base_kernel, base_scale, wave_kernels, wave_scale):
    base = (base_scale[:, None, None] * base_kernel).reshape(PLANES, 25).T[:, :, None]
    waves = (wave_scale[..., None, None] * wave_kernels).reshape(3, PLANES, 4, 25).transpose(0, 2, 3, 1)[..., None]
    lane = jnp.arange(128)[None, None, :]

    def choose(level, period, bands):
        table = jnp.zeros((25, PLANES, 128), F32)
        for residue, band in bands:
            table = jnp.where(lane % period == residue, waves[level, band], table)
        return table

    tables = [
        jnp.broadcast_to(base, (25, PLANES, 128)),
        choose(0, 2, ((0, 0), (1, 1))),
        choose(0, 2, ((0, 2), (1, 3))),
        choose(1, 4, ((0, 0), (2, 1), (1, 2), (3, 3))),
        choose(2, 8, ((0, 0), (4, 1), (1, 2), (5, 3))),
    ]
    return over_halves(jnp.concatenate(tables, 0))


def on_device(
    feature_map,
    base_kernel,
    base_bias,
    base_scale,
    wave_kernels,
    wave_scale,
    norm_gain,
    norm_bias,
    w_in,
    b_in,
    w_out,
    b_out,
    layer_scale,
    cotangent,
):
    group = ("hi", "col", "core")
    everyone = ("x", "y", "hi", "col", "core")
    core_here = lax.axis_index("core")
    place = lax.axis_index("hi") * 8 + lax.axis_index("col") * 2 + core_here
    x_here = lax.axis_index("x")
    y_here = lax.axis_index("y")

    tiles = lax.all_to_all(
        feature_map.reshape(GROUP, PLANES, 16, 128), group, split_axis=0, concat_axis=0, tiled=True
    )
    share = CHANS // (X * Y)
    norms = jnp.concatenate([norm_gain, norm_bias]).reshape(1, 2 * share)
    other = lax.ppermute(norms, "y", [(0, 1), (1, 0)])
    order = jnp.stack([x_here, core_here]).astype(jnp.int32)
    scaled, mine, others = call(
        prepare_kernel,
        (
            jax.ShapeDtypeStruct((X * Y, LINES, share, LINE), BF16),
            jax.ShapeDtypeStruct((CHANS + 16, HID), BF16),
            jax.ShapeDtypeStruct((CHANS + 16, HID), BF16),
        ),
        [],
        (
            order,
            cotangent,
            jnp.broadcast_to(layer_scale[:, None, None], (share, 1, LINE)),
            w_in,
            w_out,
            b_in.reshape(1, HID),
            norms,
            other,
        ),
        1,
    )
    mine = [mine] + [lax.ppermute(mine, "x", [(i, i ^ step) for i in range(X)]) for step in range(1, X)]
    others = [others] + [lax.ppermute(one, "core", [(0, 1), (1, 0)]) for one in mine[1:]]
    scaled = lax.all_to_all(scaled, ("x", "y"), split_axis=0, concat_axis=0, tiled=True)

    scale_own = own_planes(base_scale, 0, place)
    taps = tap_table(
        own_planes(base_kernel, 0, place),
        scale_own,
        own_planes(wave_kernels, 1, place),
        own_planes(wave_scale, 1, place),
    )

    def rows_of(vector):
        return over_halves(jnp.broadcast_to(vector[:, None], (PLANES, COLS)))

    layer = rows_of(own_planes(layer_scale, 0, place))
    sent = call(
        forward_kernel,
        jax.ShapeDtypeStruct((X, Y, GROUP, 2 * SUB, LINE), BF16),
        plane_scratch(),
        (tiles, taps, rows_of(scale_own * own_planes(base_bias, 0, place))),
        6,
    )
    received = lax.all_to_all(
        sent.reshape(X * Y * GROUP, 2 * SUB, LINE), everyone, split_axis=0, concat_axis=0, tiled=True
    )

    extras = jnp.stack([one[CHANS : CHANS + 6] for one in mine])
    extras = jnp.sum(extras.reshape(X, 3, 2, HID).astype(F32), 1)
    biases = extras[:, 0]
    norms = extras[:, 1].reshape(X, Y, 2, share)[x_here ^ jnp.arange(X)][:, y_here ^ jnp.arange(Y)]
    vectors = norms.transpose(2, 0, 1, 3).reshape(2, CHANS)

    anywhere = pl.BlockSpec(memory_space=pl.ANY)
    nearby = pl.BlockSpec(memory_space=pltpu.VMEM)
    blocks = (X * Y * GROUP, 4 * SUB, LINE)
    pieces = (X, GROUP // 2, 8, 16, 128)
    sent, kept, given = pl.pallas_call(
        mlp_kernel,
        out_shape=tuple(jax.ShapeDtypeStruct(shape, BF16) for shape in (blocks, pieces, pieces)),
        in_specs=[pl.BlockSpec(memory_space=pltpu.SMEM)] + [nearby] * 2 + [anywhere] * 10,
        out_specs=(anywhere,) * 3,
        scratch_shapes=[
            pltpu.VMEM(received.shape, BF16),
            pltpu.VMEM(scaled.shape, BF16),
            pltpu.VMEM((X, 2, CHANS + 16, HID), BF16),
            pltpu.VMEM((CHANS, SPOTS), F32),
            pltpu.VMEM((CHANS, SPOTS), BF16),
            pltpu.VMEM((CHANS, SPOTS), F32),
            pltpu.VMEM((CHANS, SPOTS), F32),
            pltpu.VMEM(blocks, BF16),
            pltpu.VMEM(pieces, BF16),
            pltpu.VMEM(pieces, BF16),
            pltpu.SemaphoreType.DMA((10,)),
            pltpu.SemaphoreType.DMA((12,)),
        ],
        compiler_params=pltpu.CompilerParams(vmem_limit_bytes=MLP_VMEM),
    )(
        order,
        biases,
        vectors,
        received,
        scaled,
        *mine,
        *others,
    )
    received = lax.all_to_all(sent, everyone, split_axis=0, concat_axis=0, tiled=True)

    given = lax.ppermute(given, "core", [(0, 1), (1, 0)])
    parts = [summed(kept[step], given[step]) for step in range(X)]
    parts = parts[:1] + [
        lax.ppermute(parts[step], "x", [(i, i ^ step) for i in range(X)]) for step in range(1, X)
    ]

    sent = call(
        backward_kernel,
        jax.ShapeDtypeStruct((GROUP, 2 * PLANES, 16, 128), BF16),
        plane_scratch() + [pltpu.VMEM((ROWS, SUB, COLS), F32)],
        (
            received.reshape(X, Y, GROUP, 4 * SUB, LINE),
            tiles,
            taps,
            layer,
            rows_of(own_planes(b_out, 0, place)),
        ),
        6,
    )
    pieces = call(sum_kernel, jax.ShapeDtypeStruct(parts[0].shape, BF16), [], (*parts, sent[0, 0]), 1)
    pieces = lax.all_to_all(pieces, ("hi", "col"), split_axis=0, concat_axis=0, tiled=True)
    piece = summed(*[pieces[chip] for chip in range(GROUP // 2)])
    sent = jnp.concatenate([sent, jnp.broadcast_to(piece, (GROUP,) + piece.shape)], 1)
    results = lax.all_to_all(sent, group, split_axis=0, concat_axis=0, tiled=True)
    output_map, grad_map, grad_in, grad_out = call(
        finish_kernel,
        (
            jax.ShapeDtypeStruct((GROUP, PLANES, 16, 128), BF16),
            jax.ShapeDtypeStruct((GROUP, PLANES, 16, 128), BF16),
            jax.ShapeDtypeStruct((CHANS, HID), F32),
            jax.ShapeDtypeStruct((HID, CHANS), F32),
        ),
        [],
        (results, cotangent.reshape(GROUP, PLANES, 16, 128)),
        1,
    )
    output_map, grad_map = output_map.reshape(feature_map.shape), grad_map.reshape(feature_map.shape)
    return (output_map, grad_map, grad_in, grad_out)


def solution(mesh):
    grid = Mesh(mesh.devices.reshape(2, 2, 4, X, Y), ("hi", "core", "col", "x", "y"))
    chan, row = ("x", "y"), ("hi", "core")
    return jax.shard_map(
        on_device,
        mesh=grid,
        in_specs=(
            P(chan, row, "col"),
            P(chan, None, None),
            P(chan),
            P(chan),
            P(None, chan, None, None, None),
            P(None, chan, None),
            P(chan),
            P(chan),
            P(None, chan),
            P(chan),
            P(chan, None),
            P(chan),
            P(chan),
            P(chan, row, "col"),
        ),
        out_specs=(
            P(chan, row, "col"),
            P(chan, row, "col"),
            P(None, chan),
            P(chan, None),
        ),
        check_vma=False,
    )
```

```python
import jax
import jax.numpy as jnp
from jax import lax
from jax.experimental import pallas as pl
from jax.experimental.pallas import tpu as pltpu
from jax.sharding import Mesh, PartitionSpec as P

EPSILON = 1e-06
INV_ROOT_TWO = 0.7071067811865476
INV_ROOT_TWO_PI = 0.3989422804014327
F32 = jnp.float32
BF16 = jnp.bfloat16

CHANS = 512
PLANES = 4
HALVES = 2
SUB = PLANES * HALVES
ROWS = 32
COLS = 512
LINE = 128
LINES = 4
SPOTS = LINES * LINE
HID = 256
GROUP = 16
X = 4
Y = 2
PLANE_VMEM = 12 * 1024 * 1024
MLP_VMEM = 56 * 1024 * 1024


def lanes(width=COLS):
    return lax.broadcasted_iota(jnp.int32, (SUB, width), 1)


def sublanes(width=COLS):
    return lax.broadcasted_iota(jnp.int32, (SUB, width), 0)


def turn(value, shift):
    return pltpu.roll(value, shift % value.shape[1], 1)


def pair_lanes(value, step, lane):
    return jnp.where((lane & step) == 0, value + turn(value, -step), turn(value, step) - value)


def loop(count, step, body):
    def some(index, carry):
        for inner in range(step):
            body(index * step + inner)
        return carry

    if count == step:
        some(0, 0)
    else:
        lax.fori_loop(0, count // step, some, 0)


def fill_edges(ref, rows):
    low = sublanes() < PLANES
    for edge in range(2):
        ref[edge] = jnp.where(low, 0.0, pltpu.roll(ref[rows + edge], PLANES, 0))
        ref[rows + 2 + edge] = jnp.where(low, pltpu.roll(ref[2 + edge], PLANES, 0), 0.0)


def convolve(source, rows, step, taps, first, mirrored, target):
    lane = lanes()
    chunk = 4

    def do_chunk(index):
        base = index * chunk
        totals = [None] * chunk
        for move in range(5):
            coefs = []
            for tap_row in range(5):
                place = tap_row * 5 + move
                coefs.append(taps[first + (24 - place if mirrored else place)])
            blocks = [[None] * (COLS // 128) for _ in range(chunk)]
            for block in range(COLS // 128):
                for row in range(chunk + 4):
                    value = source[base + row, :, block * 128 : block * 128 + 128]
                    for out in range(max(0, row - 4), min(chunk, row + 1)):
                        term = coefs[row - out] * value
                        blocks[out][block] = term if blocks[out][block] is None else blocks[out][block] + term
            offset = (move - 2) * step
            for out in range(chunk):
                summed = jnp.concatenate(blocks[out], 1)
                if offset:
                    kept = (lane < COLS - offset) if offset > 0 else (lane >= -offset)
                    summed = jnp.where(kept, turn(summed, -offset), 0.0)
                totals[out] = summed if totals[out] is None else totals[out] + summed
        for out in range(chunk):
            target[base + out] = totals[out]

    loop(rows // chunk, 1, do_chunk)


def wavelet(plane, taps, mirrored, level_1, level_2, level_3, conv_0, conv_1, conv_2, conv_3):
    lane = lanes()
    fill_edges(plane, ROWS)

    def split_1(row):
        upper, lower = plane[2 + 2 * row], plane[3 + 2 * row]
        level_1[0, 2 + row] = pair_lanes(0.5 * (upper + lower), 1, lane)
        level_1[1, 2 + row] = pair_lanes(0.5 * (upper - lower), 1, lane)

    loop(ROWS // 2, 4, split_1)
    fill_edges(level_1.at[0], ROWS // 2)
    fill_edges(level_1.at[1], ROWS // 2)

    for source, target, rows, step in ((level_1.at[0], level_2, ROWS // 4, 2), (level_2, level_3, ROWS // 8, 4)):
        for row in range(rows):
            upper, lower = source[2 + 2 * row], source[3 + 2 * row]
            across = pair_lanes(0.5 * (upper + lower), step, lane)
            down = pair_lanes(0.5 * (upper - lower), step, lane)
            target[2 + row] = jnp.where((lane & (step - 1)) == 0, across, turn(down, 1))
        fill_edges(target, rows)

    convolve(plane, ROWS, 1, taps, 0, mirrored, conv_0)
    convolve(level_1.at[0], ROWS // 2, 2, taps, 25, mirrored, conv_1.at[0])
    convolve(level_1.at[1], ROWS // 2, 2, taps, 50, mirrored, conv_1.at[1])
    convolve(level_2, ROWS // 4, 4, taps, 75, mirrored, conv_2)
    convolve(level_3, ROWS // 8, 8, taps, 100, mirrored, conv_3)

    for source, target, rows, step in ((conv_3, conv_2, ROWS // 8, 4), (conv_2, conv_1.at[0], ROWS // 4, 2)):
        for row in range(rows):
            kept = source[row]
            moved = turn(kept, -1)
            for half, value in ((0, kept + moved), (1, kept - moved)):
                merged = pair_lanes(0.5 * value, step, lane)
                place = 2 * row + half
                target[place] = target[place] + jnp.where((lane & (step - 1)) == 0, merged, 0.0)


def merged_rows(row, conv_1, lane):
    across, down = conv_1[0, row], conv_1[1, row]
    return pair_lanes(0.5 * (across + down), 1, lane), pair_lanes(0.5 * (across - down), 1, lane)


def tile_of(half, row_block, col):
    return (half * 4 + col) * 2 + row_block


def tile_in(tiles, row_block, col):
    parts = [tiles[tile_of(half, row_block, col)].astype(F32) for half in range(HALVES)]
    return jnp.swapaxes(jnp.concatenate(parts, 0), 0, 1)


def regroup(first, second, low):
    return (
        jnp.where(low, first, pltpu.roll(second, PLANES, 0)),
        jnp.where(low, pltpu.roll(first, PLANES, 0), second),
    )


def forward_kernel(tiles, taps, shift, sent, plane, level_1, level_2, level_3, conv_0, conv_1, conv_2, conv_3):
    for row_block in range(2):
        for col in range(4):
            cols = slice(col * LINE, col * LINE + LINE)
            plane[2 + row_block * 16 : 18 + row_block * 16, :, cols] = tile_in(tiles, row_block, col)
    wavelet(plane, taps, False, level_1, level_2, level_3, conv_0, conv_1, conv_2, conv_3)
    lane = lanes()
    bias = shift[...]
    low = sublanes(LINE) < PLANES

    def finish(group):
        rows = []
        for pair in range(LINES // 2):
            merged = merged_rows(2 * group + pair, conv_1, lane)
            for half in range(2):
                rows.append(conv_0[LINES * group + 2 * pair + half] + bias + merged[half])
        for col in range(4):
            cols = slice(col * LINE, col * LINE + LINE)
            pairs = [regroup(rows[q][:, cols], rows[q + 1][:, cols], low) for q in (0, 2)]
            for half in range(HALVES):
                block = jnp.concatenate([pairs[0][half], pairs[1][half]], 0).astype(BF16)
                for twin in range(Y):
                    sent[group % X, twin, tile_of(half, group // X, col)] = block

    loop(ROWS // LINES, 2, finish)


def backward_kernel(
    parts, tiles, taps, scale, shift, sent, plane, level_1, level_2, level_3, conv_0, conv_1, conv_2, conv_3, second
):
    low = sublanes(LINE) < PLANES

    def gather(group):
        for col in range(4):
            cols = slice(col * LINE, col * LINE + LINE)
            both = []
            for half in range(HALVES):
                place = tile_of(half, group // X, col)
                both.append(parts[group % X, 0, place].astype(F32) + parts[group % X, 1, place].astype(F32))
            for start, target, first in ((0, second, 0), (2 * SUB, plane, 2)):
                for pair in range(LINES // 2):
                    area = slice(start + pair * SUB, start + pair * SUB + SUB)
                    rows = regroup(both[0][area], both[1][area], low)
                    for half in range(2):
                        target[first + LINES * group + 2 * pair + half, :, cols] = rows[half]

    loop(ROWS // LINES, 2, gather)
    wavelet(plane, taps, True, level_1, level_2, level_3, conv_0, conv_1, conv_2, conv_3)
    lane = lanes()

    def finish(pair):
        rows = merged_rows(pair, conv_1, lane)
        for half in range(2):
            row = 2 * pair + half
            conv_0[row] = conv_0[row] + rows[half]

    loop(ROWS // 2, 4, finish)
    layer, bias = scale[...], shift[...]
    for row_block in range(2):
        for col in range(4):
            cols = slice(col * LINE, col * LINE + LINE)
            rows = slice(row_block * 16, row_block * 16 + 16)
            projected = layer[:, cols] * (second[rows, :, cols] + bias[:, cols])
            output = tile_in(tiles, row_block, col) + projected
            for first, value in ((0, output), (PLANES, conv_0[rows, :, cols])):
                turned = jnp.swapaxes(value, 0, 1).astype(BF16)
                for half in range(HALVES):
                    place = tile_of(half, row_block, col)
                    sent[place, first : first + PLANES] = turned[half * PLANES : half * PLANES + PLANES]


def plane_scratch():
    return [
        pltpu.VMEM((ROWS + 4, SUB, COLS), F32),
        pltpu.VMEM((2, ROWS // 2 + 4, SUB, COLS), F32),
        pltpu.VMEM((ROWS // 4 + 4, SUB, COLS), F32),
        pltpu.VMEM((ROWS // 8 + 4, SUB, COLS), F32),
        pltpu.VMEM((ROWS, SUB, COLS), F32),
        pltpu.VMEM((2, ROWS // 2, SUB, COLS), F32),
        pltpu.VMEM((ROWS // 4, SUB, COLS), F32),
        pltpu.VMEM((ROWS // 8, SUB, COLS), F32),
    ]


def dot(left, right, left_dim, right_dim):
    return lax.dot_general(left, right, (((left_dim,), (right_dim,)), ((), ())), preferred_element_type=F32)


def hidden_parts(pack, core, bias, normed_turned, scaled_turned):
    mine, others = pack[0, :CHANS], pack[1, :CHANS]
    w_in = jnp.where(core == 0, mine, others)
    w_out = jnp.where(core == 0, others, mine)
    w_out = jnp.concatenate([w_out[:HID], w_out[HID:]], 1).T
    hidden = dot(normed_turned, w_in, 1, 0) + bias
    spread = 0.5 * (1.0 + lax.erf(hidden * INV_ROOT_TWO))
    activated = (hidden * spread).astype(BF16)
    slope = spread + hidden * jnp.exp(-0.5 * hidden * hidden) * INV_ROOT_TWO_PI
    grad_hidden = (dot(scaled_turned, w_out, 1, 0) * slope).astype(BF16)
    return w_in, w_out, activated, grad_hidden


def mlp_kernel(
    order, biases, vectors, received_at, twins,
    mine_0, mine_1, mine_2, mine_3, others_0, others_1, others_2, others_3, sent_at, kept_at, given_at,
    received, received_scaled, packs, mixed, scaled, projected, grads, sent, kept, given, arrived, left,
):
    halves = ((mine_0, others_0), (mine_1, others_1), (mine_2, others_2), (mine_3, others_3))
    share = CHANS // (X * Y)
    blocks = [pair[0].at[CHANS + 16 : CHANS + 16 + 2 * share] for pair in halves]
    sources = (received_at, *blocks, twins, *[half.at[:CHANS] for pair in halves for half in pair])
    targets = (
        received,
        *[received_scaled.at[0, index] for index in range(X)],
        received_scaled.at[1],
        *[packs.at[index, half] for index in range(X) for half in range(2)],
    )
    arrivals = [
        pltpu.make_async_copy(source, target, arrived.at[i]) for i, (source, target) in enumerate(zip(sources, targets))
    ]
    for copy in arrivals:
        copy.start()
    departures = []

    def depart(source, target):
        copy = pltpu.make_async_copy(source, target, left.at[len(departures)])
        copy.start()
        departures.append(copy)

    arrivals[0].wait()
    low = sublanes(LINE) < PLANES

    def arrange(index):
        for pair in range(2):
            one = received[4 * index + 2 * pair].astype(F32)
            two = received[4 * index + 2 * pair + 1].astype(F32)
            rows = pl.ds(pl.multiple_of(index * 16 + pair * SUB, SUB), SUB)
            for half in range(2):
                area = slice(half * SUB, half * SUB + SUB)
                lines = regroup(one[area], two[area], low)
                for line in range(2):
                    place = (2 * half + line) * LINE
                    mixed[rows, place : place + LINE] = lines[line]

    loop(CHANS // 16, 4, arrange)
    for index in range(X + 1):
        arrivals[1 + index].wait()
    for index in range(X):
        for twin in range(Y):
            chip = (order[0] ^ index) * Y + (order[2] ^ twin)
            rows = pl.ds(pl.multiple_of(chip * share, share), share)
            for pair in range(LINES // 2):
                area = slice(pair * share, pair * share + share)
                scaled[rows, pair * 2 * LINE : (pair + 1) * 2 * LINE] = received_scaled[twin, index, area]
    values = mixed[...]
    average = jnp.sum(values, 0, keepdims=True) / CHANS
    rescale = lax.rsqrt(jnp.sum(values * values, 0, keepdims=True) / CHANS - average * average + EPSILON)
    gains, shifts = [
        jnp.concatenate([jnp.broadcast_to(vectors[row : row + 1], (LINE, CHANS)).T] * (SPOTS // LINE), 1)
        for row in range(2)
    ]
    normed = (((values - average) * rescale) * gains + shifts).astype(BF16)
    scaled_now = scaled[...]
    normed_turned, scaled_turned = normed.T, scaled_now.T
    for index in range(X):
        arrivals[6 + 2 * index].wait()
        arrivals[7 + 2 * index].wait()
        w_in, w_out, activated, grad_hidden = hidden_parts(
            packs.at[index], order[1], biases[index : index + 1], normed_turned, scaled_turned
        )
        part = dot(w_out, activated, 1, 1)
        projected[...] = part if index == 0 else projected[...] + part
        part = dot(w_in, grad_hidden, 1, 1)
        grads[...] = part if index == 0 else grads[...] + part
        for arr, value in ((0, dot(normed, grad_hidden, 1, 0)), (1, dot(scaled_now, activated, 1, 0))):
            rounded = value.astype(BF16)
            for piece in range(GROUP // 2):
                first, second = rounded[piece * 64 : piece * 64 + 32], rounded[piece * 64 + 32 : piece * 64 + 64]
                for part in range(4):
                    cut = (slice(part % 2 * 16, part % 2 * 16 + 16), slice(part // 2 * 128, part // 2 * 128 + 128))
                    kept[index, piece, arr * 4 + part] = jnp.where(order[1] == 0, first[cut], second[cut])
                    given[index, piece, arr * 4 + part] = jnp.where(order[1] == 0, second[cut], first[cut])
        depart(given.at[index], given_at.at[index])
        depart(kept.at[index], kept_at.at[index])
    weighted = grads[...] * gains
    centred = (mixed[...] - average) * rescale
    sum_one = jnp.sum(weighted, 0, keepdims=True) / CHANS
    sum_two = jnp.sum(weighted * centred, 0, keepdims=True) / CHANS
    grads[...] = rescale * (weighted - sum_one - centred * sum_two)

    def hand_out(index):
        rows = pl.ds(pl.multiple_of(index * SUB, SUB), SUB)
        blocks = [[], []]
        for ref in (projected, grads):
            value = ref[rows]
            for half in range(2):
                place = 2 * half * LINE
                pair = regroup(value[:, place : place + LINE], value[:, place + LINE : place + 2 * LINE], low)
                for which in range(2):
                    blocks[which].append(pair[which])
        for which in range(2):
            sent[2 * index + which] = jnp.concatenate(blocks[which], 0).astype(BF16)

    quarter = CHANS // SUB // 4
    for part in range(4):
        loop(quarter, 4, lambda index: hand_out(part * quarter + index))
        area = pl.ds(part * 2 * quarter, 2 * quarter)
        depart(sent.at[area], sent_at.at[area])
    for copy in departures:
        copy.wait()


def sum_kernel(first, second, third, fourth, after, total):
    for place in range(first.shape[0]):
        parts = [ref[place].astype(F32) for ref in (first, second, third, fourth)]
        total[place] = (parts[0] + parts[1] + parts[2] + parts[3]).astype(BF16)


def finish_kernel(results, cotangent, output_map, grad_map, grad_in, grad_out):
    output_map[...] = results[:, :PLANES]
    grad_map[...] = (cotangent[...].astype(F32) + results[:, PLANES : 2 * PLANES].astype(F32)).astype(BF16)
    factor = 1.0 / (64.0 * 512.0) ** 0.5
    for half in range(2):
        cols = slice(half * 128, half * 128 + 128)
        for pair in range(GROUP // 4):
            blocks = []
            for piece in range(4 * pair, 4 * pair + 4):
                for part in range(2):
                    rows = slice(piece * 32 + part * 16, piece * 32 + part * 16 + 16)
                    grad_in[rows, cols] = results[piece, 2 * PLANES + half * 2 + part].astype(F32) * factor
                    blocks.append(results[piece, 2 * PLANES + 4 + half * 2 + part])
            block = jnp.concatenate(blocks, 0).astype(F32) * factor
            grad_out[cols, pair * 128 : pair * 128 + 128] = block.T


def call(kernel, outs, scratch, ops, microseconds):
    spaces = [
        pl.BlockSpec(memory_space=pltpu.SMEM if op.dtype == jnp.int32 else pltpu.VMEM) for op in ops
    ]
    out_spaces = jax.tree.map(lambda _: pl.BlockSpec(memory_space=pltpu.VMEM), outs)
    return pl.pallas_call(
        kernel,
        out_shape=outs,
        in_specs=spaces,
        out_specs=out_spaces,
        scratch_shapes=scratch,
        compiler_params=pltpu.CompilerParams(vmem_limit_bytes=PLANE_VMEM),
        cost_estimate=pl.CostEstimate(flops=0, bytes_accessed=int(microseconds * 3.5e6), transcendentals=0),
    )(*ops)


def scale_kernel(cotangent, layer, scaled):
    for block in range(0, CHANS // (X * Y), 16):
        rows = [
            jnp.swapaxes(cotangent[part : part + SUB].astype(F32) * layer[part : part + SUB], 0, 1)
            for part in (block, block + SUB)
        ]
        scaled[:, block : block + 16] = jnp.concatenate(rows, 1).astype(BF16)


def prepare_kernel(
    order, w_in, w_out, b_in, norms, other, scaled, pack_0, pack_1, pack_2, pack_3, others
):
    packs = (pack_0, pack_1, pack_2, pack_3)
    for half in range(2):
        area = slice(half * HID, half * HID + HID)
        first, second = w_in[area], w_out[:, area]
        mine = jnp.where(order[1] == 0, first, second)
        for pack in packs:
            pack[area] = mine
        others[area] = jnp.where(order[1] == 0, second, first)
    left = [b_in[...], jnp.concatenate([norms[...], other[...]], 1)]
    rows = []
    for _ in range(3):
        parts = [value.astype(BF16).astype(F32) for value in left]
        left = [value - part for value, part in zip(left, parts)]
        rows.extend(parts)
    small = jnp.concatenate(rows + [jnp.zeros((10, HID), F32)], 0).astype(BF16)
    share = CHANS // (X * Y)
    for step, pack in enumerate(packs):
        pack[CHANS : CHANS + 16] = small
        start = (order[0] ^ step) * LINES
        for pair in range(LINES // 2):
            first = CHANS + 16 + pair * share
            lines = (scaled[start + 2 * pair], scaled[start + 2 * pair + 1])
            pack[first : first + share] = jnp.concatenate(lines, 1)


def summed(*terms):
    total = terms[0].astype(F32)
    for term in terms[1:]:
        total = total + term.astype(F32)
    return total.astype(BF16)


def own_planes(array, dim, place):
    return lax.dynamic_slice_in_dim(array, place * PLANES, PLANES, dim)


def over_halves(array):
    return jnp.concatenate([array, array], -2)


def tap_table(base_kernel, base_scale, wave_kernels, wave_scale):
    base = (base_scale[:, None, None] * base_kernel).reshape(PLANES, 25).T[:, :, None]
    waves = (wave_scale[..., None, None] * wave_kernels).reshape(3, PLANES, 4, 25).transpose(0, 2, 3, 1)[..., None]
    lane = jnp.arange(128)[None, None, :]

    def choose(level, period, bands):
        table = jnp.zeros((25, PLANES, 128), F32)
        for residue, band in bands:
            table = jnp.where(lane % period == residue, waves[level, band], table)
        return table

    tables = [
        jnp.broadcast_to(base, (25, PLANES, 128)),
        choose(0, 2, ((0, 0), (1, 1))),
        choose(0, 2, ((0, 2), (1, 3))),
        choose(1, 4, ((0, 0), (2, 1), (1, 2), (3, 3))),
        choose(2, 8, ((0, 0), (4, 1), (1, 2), (5, 3))),
    ]
    return over_halves(jnp.concatenate(tables, 0))


def on_device(
    feature_map,
    base_kernel,
    base_bias,
    base_scale,
    wave_kernels,
    wave_scale,
    norm_gain,
    norm_bias,
    w_in,
    b_in,
    w_out,
    b_out,
    layer_scale,
    cotangent,
):
    group = ("hi", "col", "core")
    everyone = ("x", "y", "hi", "col", "core")
    core_here = lax.axis_index("core")
    place = lax.axis_index("hi") * 8 + lax.axis_index("col") * 2 + core_here
    x_here = lax.axis_index("x")
    y_here = lax.axis_index("y")

    tiles = lax.all_to_all(
        feature_map.reshape(GROUP, PLANES, 16, 128), group, split_axis=0, concat_axis=0, tiled=True
    )
    share = CHANS // (X * Y)
    norms = jnp.concatenate([norm_gain, norm_bias]).reshape(1, 2 * share)
    other = lax.ppermute(norms, "y", [(0, 1), (1, 0)])
    order = jnp.stack([x_here, core_here, y_here]).astype(jnp.int32)
    scaled = call(
        scale_kernel,
        jax.ShapeDtypeStruct((16, share, LINE), BF16),
        [],
        (cotangent, jnp.broadcast_to(layer_scale[:, None, None], (share, 1, LINE))),
        1,
    )
    *mine, others = call(
        prepare_kernel,
        (jax.ShapeDtypeStruct((CHANS + 16 + 2 * share, HID), BF16),) * X + (jax.ShapeDtypeStruct((CHANS, HID), BF16),),
        [],
        (order, w_in, w_out, b_in.reshape(1, HID), norms, other, scaled),
        1,
    )
    mine = mine[:1] + [lax.ppermute(mine[step], "x", [(i, i ^ step) for i in range(X)]) for step in range(1, X)]
    others = [others] + [lax.ppermute(one[:CHANS], "core", [(0, 1), (1, 0)]) for one in mine[1:]]
    twins = lax.ppermute(jnp.stack([one[CHANS + 16 :] for one in mine]), "y", [(0, 1), (1, 0)])

    scale_own = own_planes(base_scale, 0, place)
    taps = tap_table(
        own_planes(base_kernel, 0, place),
        scale_own,
        own_planes(wave_kernels, 1, place),
        own_planes(wave_scale, 1, place),
    )

    def rows_of(vector):
        return over_halves(jnp.broadcast_to(vector[:, None], (PLANES, COLS)))

    layer = rows_of(own_planes(layer_scale, 0, place))
    sent = call(
        forward_kernel,
        jax.ShapeDtypeStruct((X, Y, GROUP, 2 * SUB, LINE), BF16),
        plane_scratch(),
        (tiles, taps, rows_of(scale_own * own_planes(base_bias, 0, place))),
        6,
    )
    received = lax.all_to_all(
        sent.reshape(X * Y * GROUP, 2 * SUB, LINE), everyone, split_axis=0, concat_axis=0, tiled=True
    )

    extras = jnp.stack([one[CHANS : CHANS + 6] for one in mine])
    extras = jnp.sum(extras.reshape(X, 3, 2, HID).astype(F32), 1)
    biases = extras[:, 0]
    norms = extras[:, 1].reshape(X, Y, 2, share)[x_here ^ jnp.arange(X)][:, y_here ^ jnp.arange(Y)]
    vectors = norms.transpose(2, 0, 1, 3).reshape(2, CHANS)

    anywhere = pl.BlockSpec(memory_space=pl.ANY)
    nearby = pl.BlockSpec(memory_space=pltpu.VMEM)
    blocks = (X * Y * GROUP, 4 * SUB, LINE)
    pieces = (X, GROUP // 2, 8, 16, 128)
    sent, kept, given = pl.pallas_call(
        mlp_kernel,
        out_shape=tuple(jax.ShapeDtypeStruct(shape, BF16) for shape in (blocks, pieces, pieces)),
        in_specs=[pl.BlockSpec(memory_space=pltpu.SMEM)] + [nearby] * 2 + [anywhere] * 10,
        out_specs=(anywhere,) * 3,
        scratch_shapes=[
            pltpu.VMEM(received.shape, BF16),
            pltpu.VMEM((Y, X, 2 * share, HID), BF16),
            pltpu.VMEM((X, 2, CHANS, HID), BF16),
            pltpu.VMEM((CHANS, SPOTS), F32),
            pltpu.VMEM((CHANS, SPOTS), BF16),
            pltpu.VMEM((CHANS, SPOTS), F32),
            pltpu.VMEM((CHANS, SPOTS), F32),
            pltpu.VMEM(blocks, BF16),
            pltpu.VMEM(pieces, BF16),
            pltpu.VMEM(pieces, BF16),
            pltpu.SemaphoreType.DMA((14,)),
            pltpu.SemaphoreType.DMA((12,)),
        ],
        compiler_params=pltpu.CompilerParams(vmem_limit_bytes=MLP_VMEM),
    )(
        order,
        biases,
        vectors,
        received,
        twins,
        *mine,
        *others,
    )
    received = lax.all_to_all(sent, everyone, split_axis=0, concat_axis=0, tiled=True)

    given = lax.ppermute(given, "core", [(0, 1), (1, 0)])
    parts = [summed(kept[step], given[step]) for step in range(X)]
    parts = parts[:1] + [
        lax.ppermute(parts[step], "x", [(i, i ^ step) for i in range(X)]) for step in range(1, X)
    ]

    sent = call(
        backward_kernel,
        jax.ShapeDtypeStruct((GROUP, 2 * PLANES, 16, 128), BF16),
        plane_scratch() + [pltpu.VMEM((ROWS, SUB, COLS), F32)],
        (
            received.reshape(X, Y, GROUP, 4 * SUB, LINE),
            tiles,
            taps,
            layer,
            rows_of(own_planes(b_out, 0, place)),
        ),
        6,
    )
    pieces = call(sum_kernel, jax.ShapeDtypeStruct(parts[0].shape, BF16), [], (*parts, sent[0, 0]), 1)
    pieces = lax.all_to_all(pieces, ("hi", "col"), split_axis=0, concat_axis=0, tiled=True)
    piece = summed(*[pieces[chip] for chip in range(GROUP // 2)])
    sent = jnp.concatenate([sent, jnp.broadcast_to(piece, (GROUP,) + piece.shape)], 1)
    results = lax.all_to_all(sent, group, split_axis=0, concat_axis=0, tiled=True)
    output_map, grad_map, grad_in, grad_out = call(
        finish_kernel,
        (
            jax.ShapeDtypeStruct((GROUP, PLANES, 16, 128), BF16),
            jax.ShapeDtypeStruct((GROUP, PLANES, 16, 128), BF16),
            jax.ShapeDtypeStruct((CHANS, HID), F32),
            jax.ShapeDtypeStruct((HID, CHANS), F32),
        ),
        [],
        (results, cotangent.reshape(GROUP, PLANES, 16, 128)),
        1,
    )
    output_map, grad_map = output_map.reshape(feature_map.shape), grad_map.reshape(feature_map.shape)
    return (output_map, grad_map, grad_in, grad_out)


def solution(mesh):
    grid = Mesh(mesh.devices.reshape(2, 2, 4, X, Y), ("hi", "core", "col", "x", "y"))
    chan, row = ("x", "y"), ("hi", "core")
    return jax.shard_map(
        on_device,
        mesh=grid,
        in_specs=(
            P(chan, row, "col"),
            P(chan, None, None),
            P(chan),
            P(chan),
            P(None, chan, None, None, None),
            P(None, chan, None),
            P(chan),
            P(chan),
            P(None, chan),
            P(chan),
            P(chan, None),
            P(chan),
            P(chan),
            P(chan, row, "col"),
        ),
        out_specs=(
            P(chan, row, "col"),
            P(chan, row, "col"),
            P(None, chan),
            P(chan, None),
        ),
        check_vma=False,
    )
```

```python
import jax
import jax.numpy as jnp
from jax import lax
from jax.experimental import pallas as pl
from jax.experimental.pallas import tpu as pltpu
from jax.sharding import Mesh, PartitionSpec as P

EPSILON = 1e-06
INV_ROOT_TWO = 0.7071067811865476
INV_ROOT_TWO_PI = 0.3989422804014327
F32 = jnp.float32
BF16 = jnp.bfloat16

CHANS = 512
PLANES = 4
HALVES = 2
SUB = PLANES * HALVES
ROWS = 32
COLS = 512
LINE = 128
LINES = 4
SPOTS = LINES * LINE
HID = 256
GROUP = 16
X = 4
Y = 2
PLANE_VMEM = 12 * 1024 * 1024
MLP_VMEM = 56 * 1024 * 1024


def lanes(width=COLS):
    return lax.broadcasted_iota(jnp.int32, (SUB, width), 1)


def sublanes(width=COLS):
    return lax.broadcasted_iota(jnp.int32, (SUB, width), 0)


def turn(value, shift):
    return pltpu.roll(value, shift % value.shape[1], 1)


def pair_lanes(value, step, lane):
    return jnp.where((lane & step) == 0, value + turn(value, -step), turn(value, step) - value)


def loop(count, step, body):
    def some(index, carry):
        for inner in range(step):
            body(index * step + inner)
        return carry

    if count == step:
        some(0, 0)
    else:
        lax.fori_loop(0, count // step, some, 0)


def fill_edges(ref, rows):
    low = sublanes() < PLANES
    for edge in range(2):
        ref[edge] = jnp.where(low, 0.0, pltpu.roll(ref[rows + edge], PLANES, 0))
        ref[rows + 2 + edge] = jnp.where(low, pltpu.roll(ref[2 + edge], PLANES, 0), 0.0)


def convolve(source, rows, step, taps, first, mirrored, target):
    lane = lanes()
    chunk = 4

    def do_chunk(index):
        base = index * chunk
        totals = [None] * chunk
        for move in range(5):
            coefs = []
            for tap_row in range(5):
                place = tap_row * 5 + move
                coefs.append(taps[first + (24 - place if mirrored else place)])
            blocks = [[None] * (COLS // 128) for _ in range(chunk)]
            for block in range(COLS // 128):
                for row in range(chunk + 4):
                    value = source[base + row, :, block * 128 : block * 128 + 128]
                    for out in range(max(0, row - 4), min(chunk, row + 1)):
                        term = coefs[row - out] * value
                        blocks[out][block] = term if blocks[out][block] is None else blocks[out][block] + term
            offset = (move - 2) * step
            for out in range(chunk):
                summed = jnp.concatenate(blocks[out], 1)
                if offset:
                    kept = (lane < COLS - offset) if offset > 0 else (lane >= -offset)
                    summed = jnp.where(kept, turn(summed, -offset), 0.0)
                totals[out] = summed if totals[out] is None else totals[out] + summed
        for out in range(chunk):
            target[base + out] = totals[out]

    loop(rows // chunk, 1, do_chunk)


def wavelet(plane, taps, mirrored, level_1, level_2, level_3, conv_0, conv_1, conv_2, conv_3):
    lane = lanes()
    fill_edges(plane, ROWS)

    def split_1(row):
        upper, lower = plane[2 + 2 * row], plane[3 + 2 * row]
        level_1[0, 2 + row] = pair_lanes(0.5 * (upper + lower), 1, lane)
        level_1[1, 2 + row] = pair_lanes(0.5 * (upper - lower), 1, lane)

    loop(ROWS // 2, 4, split_1)
    fill_edges(level_1.at[0], ROWS // 2)
    fill_edges(level_1.at[1], ROWS // 2)

    for source, target, rows, step in ((level_1.at[0], level_2, ROWS // 4, 2), (level_2, level_3, ROWS // 8, 4)):
        for row in range(rows):
            upper, lower = source[2 + 2 * row], source[3 + 2 * row]
            across = pair_lanes(0.5 * (upper + lower), step, lane)
            down = pair_lanes(0.5 * (upper - lower), step, lane)
            target[2 + row] = jnp.where((lane & (step - 1)) == 0, across, turn(down, 1))
        fill_edges(target, rows)

    convolve(plane, ROWS, 1, taps, 0, mirrored, conv_0)
    convolve(level_1.at[0], ROWS // 2, 2, taps, 25, mirrored, conv_1.at[0])
    convolve(level_1.at[1], ROWS // 2, 2, taps, 50, mirrored, conv_1.at[1])
    convolve(level_2, ROWS // 4, 4, taps, 75, mirrored, conv_2)
    convolve(level_3, ROWS // 8, 8, taps, 100, mirrored, conv_3)

    for source, target, rows, step in ((conv_3, conv_2, ROWS // 8, 4), (conv_2, conv_1.at[0], ROWS // 4, 2)):
        for row in range(rows):
            kept = source[row]
            moved = turn(kept, -1)
            for half, value in ((0, kept + moved), (1, kept - moved)):
                merged = pair_lanes(0.5 * value, step, lane)
                place = 2 * row + half
                target[place] = target[place] + jnp.where((lane & (step - 1)) == 0, merged, 0.0)


def merged_rows(row, conv_1, lane):
    across, down = conv_1[0, row], conv_1[1, row]
    return pair_lanes(0.5 * (across + down), 1, lane), pair_lanes(0.5 * (across - down), 1, lane)


def tile_of(half, row_block, col):
    return (half * 4 + col) * 2 + row_block


def tile_in(tiles, row_block, col):
    parts = [tiles[tile_of(half, row_block, col)].astype(F32) for half in range(HALVES)]
    return jnp.swapaxes(jnp.concatenate(parts, 0), 0, 1)


def regroup(first, second, low):
    return (
        jnp.where(low, first, pltpu.roll(second, PLANES, 0)),
        jnp.where(low, pltpu.roll(first, PLANES, 0), second),
    )


def forward_kernel(tiles, taps, shift, sent, plane, level_1, level_2, level_3, conv_0, conv_1, conv_2, conv_3):
    for row_block in range(2):
        for col in range(4):
            cols = slice(col * LINE, col * LINE + LINE)
            plane[2 + row_block * 16 : 18 + row_block * 16, :, cols] = tile_in(tiles, row_block, col)
    wavelet(plane, taps, False, level_1, level_2, level_3, conv_0, conv_1, conv_2, conv_3)
    lane = lanes()
    bias = shift[...]
    low = sublanes(LINE) < PLANES

    def finish(group):
        rows = []
        for pair in range(LINES // 2):
            merged = merged_rows(2 * group + pair, conv_1, lane)
            for half in range(2):
                rows.append(conv_0[LINES * group + 2 * pair + half] + bias + merged[half])
        for col in range(4):
            cols = slice(col * LINE, col * LINE + LINE)
            pairs = [regroup(rows[q][:, cols], rows[q + 1][:, cols], low) for q in (0, 2)]
            for half in range(HALVES):
                block = jnp.concatenate([pairs[0][half], pairs[1][half]], 0).astype(BF16)
                for twin in range(Y):
                    sent[group % X, twin, tile_of(half, group // X, col)] = block

    loop(ROWS // LINES, 2, finish)


def backward_kernel(
    parts, tiles, taps, scale, shift, sent, plane, level_1, level_2, level_3, conv_0, conv_1, conv_2, conv_3, second
):
    low = sublanes(LINE) < PLANES

    def gather(group):
        for col in range(4):
            cols = slice(col * LINE, col * LINE + LINE)
            both = []
            for half in range(HALVES):
                place = tile_of(half, group // X, col)
                both.append(parts[group % X, 0, place].astype(F32) + parts[group % X, 1, place].astype(F32))
            for start, target, first in ((0, second, 0), (2 * SUB, plane, 2)):
                for pair in range(LINES // 2):
                    area = slice(start + pair * SUB, start + pair * SUB + SUB)
                    rows = regroup(both[0][area], both[1][area], low)
                    for half in range(2):
                        target[first + LINES * group + 2 * pair + half, :, cols] = rows[half]

    loop(ROWS // LINES, 2, gather)
    wavelet(plane, taps, True, level_1, level_2, level_3, conv_0, conv_1, conv_2, conv_3)
    lane = lanes()

    def finish(pair):
        rows = merged_rows(pair, conv_1, lane)
        for half in range(2):
            row = 2 * pair + half
            conv_0[row] = conv_0[row] + rows[half]

    loop(ROWS // 2, 4, finish)
    layer, bias = scale[...], shift[...]
    for row_block in range(2):
        for col in range(4):
            cols = slice(col * LINE, col * LINE + LINE)
            rows = slice(row_block * 16, row_block * 16 + 16)
            projected = layer[:, cols] * (second[rows, :, cols] + bias[:, cols])
            output = tile_in(tiles, row_block, col) + projected
            for first, value in ((0, output), (PLANES, conv_0[rows, :, cols])):
                turned = jnp.swapaxes(value, 0, 1).astype(BF16)
                for half in range(HALVES):
                    place = tile_of(half, row_block, col)
                    sent[place, first : first + PLANES] = turned[half * PLANES : half * PLANES + PLANES]


def plane_scratch():
    return [
        pltpu.VMEM((ROWS + 4, SUB, COLS), F32),
        pltpu.VMEM((2, ROWS // 2 + 4, SUB, COLS), F32),
        pltpu.VMEM((ROWS // 4 + 4, SUB, COLS), F32),
        pltpu.VMEM((ROWS // 8 + 4, SUB, COLS), F32),
        pltpu.VMEM((ROWS, SUB, COLS), F32),
        pltpu.VMEM((2, ROWS // 2, SUB, COLS), F32),
        pltpu.VMEM((ROWS // 4, SUB, COLS), F32),
        pltpu.VMEM((ROWS // 8, SUB, COLS), F32),
    ]


def dot(left, right, left_dim, right_dim):
    return lax.dot_general(left, right, (((left_dim,), (right_dim,)), ((), ())), preferred_element_type=F32)


def hidden_parts(pack, core, bias, normed_turned, scaled_turned):
    mine, others = pack[0, :CHANS], pack[1, :CHANS]
    w_in = jnp.where(core == 0, mine, others)
    w_out = jnp.where(core == 0, others, mine)
    w_out = jnp.concatenate([w_out[:HID], w_out[HID:]], 1).T
    hidden = dot(normed_turned, w_in, 1, 0) + bias
    spread = 0.5 * (1.0 + lax.erf(hidden * INV_ROOT_TWO))
    activated = (hidden * spread).astype(BF16)
    slope = spread + hidden * jnp.exp(-0.5 * hidden * hidden) * INV_ROOT_TWO_PI
    grad_hidden = (dot(scaled_turned, w_out, 1, 0) * slope).astype(BF16)
    return w_in, w_out, activated, grad_hidden


def mlp_kernel(
    order, biases, vectors, received_at, twins,
    mine_0, mine_1, mine_2, mine_3, others_0, others_1, others_2, others_3, sent_at, kept_at, given_at,
    received, received_scaled, packs, mixed, scaled, projected, grads, sent, kept, given, arrived, left,
):
    halves = ((mine_0, others_0), (mine_1, others_1), (mine_2, others_2), (mine_3, others_3))
    share = CHANS // (X * Y)
    blocks = [pair[0].at[CHANS + 16 : CHANS + 16 + 2 * share] for pair in halves]
    sources = (received_at, *blocks, twins, *[half.at[:CHANS] for pair in halves for half in pair])
    targets = (
        received,
        *[received_scaled.at[0, index] for index in range(X)],
        received_scaled.at[1],
        *[packs.at[index, half] for index in range(X) for half in range(2)],
    )
    arrivals = [
        pltpu.make_async_copy(source, target, arrived.at[i]) for i, (source, target) in enumerate(zip(sources, targets))
    ]
    for copy in arrivals:
        copy.start()
    departures = []

    def depart(source, target):
        copy = pltpu.make_async_copy(source, target, left.at[len(departures)])
        copy.start()
        departures.append(copy)

    arrivals[0].wait()
    low = sublanes(LINE) < PLANES

    def arrange(index):
        for pair in range(2):
            one = received[4 * index + 2 * pair].astype(F32)
            two = received[4 * index + 2 * pair + 1].astype(F32)
            rows = pl.ds(pl.multiple_of(index * 16 + pair * SUB, SUB), SUB)
            for half in range(2):
                area = slice(half * SUB, half * SUB + SUB)
                lines = regroup(one[area], two[area], low)
                for line in range(2):
                    place = (2 * half + line) * LINE
                    mixed[rows, place : place + LINE] = lines[line]

    loop(CHANS // 16, 4, arrange)
    for index in range(X + 1):
        arrivals[1 + index].wait()
    for index in range(X):
        for twin in range(Y):
            chip = (order[0] ^ index) * Y + (order[2] ^ twin)
            rows = pl.ds(pl.multiple_of(chip * share, share), share)
            for pair in range(LINES // 2):
                area = slice(pair * share, pair * share + share)
                scaled[rows, pair * 2 * LINE : (pair + 1) * 2 * LINE] = received_scaled[twin, index, area]
    values = mixed[...]
    average = jnp.sum(values, 0, keepdims=True) / CHANS
    rescale = lax.rsqrt(jnp.sum(values * values, 0, keepdims=True) / CHANS - average * average + EPSILON)
    gains, shifts = [
        jnp.concatenate([jnp.broadcast_to(vectors[row : row + 1], (LINE, CHANS)).T] * (SPOTS // LINE), 1)
        for row in range(2)
    ]
    normed = (((values - average) * rescale) * gains + shifts).astype(BF16)
    scaled_now = scaled[...]
    normed_turned, scaled_turned = normed.T, scaled_now.T
    for index in range(X):
        arrivals[6 + 2 * index].wait()
        arrivals[7 + 2 * index].wait()
        w_in, w_out, activated, grad_hidden = hidden_parts(
            packs.at[index], order[1], biases[index : index + 1], normed_turned, scaled_turned
        )
        part = dot(w_out, activated, 1, 1)
        projected[...] = part if index == 0 else projected[...] + part
        part = dot(w_in, grad_hidden, 1, 1)
        grads[...] = part if index == 0 else grads[...] + part
        for arr, value in ((0, dot(normed, grad_hidden, 1, 0)), (1, dot(scaled_now, activated, 1, 0))):
            rounded = value.astype(BF16)
            for piece in range(GROUP // 2):
                first, second = rounded[piece * 64 : piece * 64 + 32], rounded[piece * 64 + 32 : piece * 64 + 64]
                for part in range(4):
                    cut = (slice(part % 2 * 16, part % 2 * 16 + 16), slice(part // 2 * 128, part // 2 * 128 + 128))
                    kept[index, piece, arr * 4 + part] = jnp.where(order[1] == 0, first[cut], second[cut])
                    given[index, piece, arr * 4 + part] = jnp.where(order[1] == 0, second[cut], first[cut])
        depart(given.at[index], given_at.at[index])
        depart(kept.at[index], kept_at.at[index])
    weighted = grads[...] * gains
    centred = (mixed[...] - average) * rescale
    sum_one = jnp.sum(weighted, 0, keepdims=True) / CHANS
    sum_two = jnp.sum(weighted * centred, 0, keepdims=True) / CHANS
    grads[...] = rescale * (weighted - sum_one - centred * sum_two)

    def hand_out(index):
        rows = pl.ds(pl.multiple_of(index * SUB, SUB), SUB)
        blocks = [[], []]
        for ref in (projected, grads):
            value = ref[rows]
            for half in range(2):
                place = 2 * half * LINE
                pair = regroup(value[:, place : place + LINE], value[:, place + LINE : place + 2 * LINE], low)
                for which in range(2):
                    blocks[which].append(pair[which])
        for which in range(2):
            sent[2 * index + which] = jnp.concatenate(blocks[which], 0).astype(BF16)

    quarter = CHANS // SUB // 4
    for part in range(4):
        loop(quarter, 4, lambda index: hand_out(part * quarter + index))
        area = pl.ds(part * 2 * quarter, 2 * quarter)
        depart(sent.at[area], sent_at.at[area])
    for copy in departures:
        copy.wait()


def sum_kernel(first, second, third, fourth, after, total):
    for place in range(first.shape[0]):
        parts = [ref[place].astype(F32) for ref in (first, second, third, fourth)]
        total[place] = (parts[0] + parts[1] + parts[2] + parts[3]).astype(BF16)


def finish_kernel(results, cotangent, output_map, grad_map, grad_in, grad_out):
    output_map[...] = results[:, :PLANES]
    grad_map[...] = (cotangent[...].astype(F32) + results[:, PLANES : 2 * PLANES].astype(F32)).astype(BF16)
    factor = 1.0 / (64.0 * 512.0) ** 0.5
    for half in range(2):
        cols = slice(half * 128, half * 128 + 128)
        for pair in range(GROUP // 4):
            blocks = []
            for piece in range(4 * pair, 4 * pair + 4):
                for part in range(2):
                    rows = slice(piece * 32 + part * 16, piece * 32 + part * 16 + 16)
                    grad_in[rows, cols] = results[piece, 2 * PLANES + half * 2 + part].astype(F32) * factor
                    blocks.append(results[piece, 2 * PLANES + 4 + half * 2 + part])
            block = jnp.concatenate(blocks, 0).astype(F32) * factor
            grad_out[cols, pair * 128 : pair * 128 + 128] = block.T


def call(kernel, outs, scratch, ops, microseconds):
    spaces = [
        pl.BlockSpec(memory_space=pltpu.SMEM if op.dtype == jnp.int32 else pltpu.VMEM) for op in ops
    ]
    out_spaces = jax.tree.map(lambda _: pl.BlockSpec(memory_space=pltpu.VMEM), outs)
    return pl.pallas_call(
        kernel,
        out_shape=outs,
        in_specs=spaces,
        out_specs=out_spaces,
        scratch_shapes=scratch,
        compiler_params=pltpu.CompilerParams(vmem_limit_bytes=PLANE_VMEM),
        cost_estimate=pl.CostEstimate(flops=0, bytes_accessed=int(microseconds * 3.5e6), transcendentals=0),
    )(*ops)


def scale_kernel(cotangent, layer, scaled):
    for block in range(0, CHANS // (X * Y), 16):
        rows = [
            jnp.swapaxes(cotangent[part : part + SUB].astype(F32) * layer[part : part + SUB], 0, 1)
            for part in (block, block + SUB)
        ]
        scaled[:, block : block + 16] = jnp.concatenate(rows, 1).astype(BF16)


def prepare_kernel(
    order, w_in, w_out, b_in, norms, other, scaled, pack_0, pack_1, pack_2, pack_3, others
):
    packs = (pack_0, pack_1, pack_2, pack_3)
    for half in range(2):
        area = slice(half * HID, half * HID + HID)
        first, second = w_in[area], w_out[:, area]
        mine = jnp.where(order[1] == 0, first, second)
        for pack in packs:
            pack[area] = mine
        others[area] = jnp.where(order[1] == 0, second, first)
    left = [b_in[...], jnp.concatenate([norms[...], other[...]], 1)]
    rows = []
    for _ in range(3):
        parts = [value.astype(BF16).astype(F32) for value in left]
        left = [value - part for value, part in zip(left, parts)]
        rows.extend(parts)
    small = jnp.concatenate(rows + [jnp.zeros((10, HID), F32)], 0).astype(BF16)
    share = CHANS // (X * Y)
    for step, pack in enumerate(packs):
        pack[CHANS : CHANS + 16] = small
        start = (order[0] ^ step) * LINES
        for pair in range(LINES // 2):
            first = CHANS + 16 + pair * share
            lines = (scaled[start + 2 * pair], scaled[start + 2 * pair + 1])
            pack[first : first + share] = jnp.concatenate(lines, 1)


def summed(*terms):
    total = terms[0].astype(F32)
    for term in terms[1:]:
        total = total + term.astype(F32)
    return total.astype(BF16)


def own_planes(array, dim, place):
    return lax.dynamic_slice_in_dim(array, place * PLANES, PLANES, dim)


def over_halves(array):
    return jnp.concatenate([array, array], -2)


def tap_table(base_kernel, base_scale, wave_kernels, wave_scale):
    base = (base_scale[:, None, None] * base_kernel).reshape(PLANES, 25).T[:, :, None]
    waves = (wave_scale[..., None, None] * wave_kernels).reshape(3, PLANES, 4, 25).transpose(0, 2, 3, 1)[..., None]
    lane = jnp.arange(128)[None, None, :]

    def choose(level, period, bands):
        table = jnp.zeros((25, PLANES, 128), F32)
        for residue, band in bands:
            table = jnp.where(lane % period == residue, waves[level, band], table)
        return table

    tables = [
        jnp.broadcast_to(base, (25, PLANES, 128)),
        choose(0, 2, ((0, 0), (1, 1))),
        choose(0, 2, ((0, 2), (1, 3))),
        choose(1, 4, ((0, 0), (2, 1), (1, 2), (3, 3))),
        choose(2, 8, ((0, 0), (4, 1), (1, 2), (5, 3))),
    ]
    return over_halves(jnp.concatenate(tables, 0))


def on_device(
    feature_map,
    base_kernel,
    base_bias,
    base_scale,
    wave_kernels,
    wave_scale,
    norm_gain,
    norm_bias,
    w_in,
    b_in,
    w_out,
    b_out,
    layer_scale,
    cotangent,
):
    group = ("hi", "col", "core")
    everyone = ("x", "y", "hi", "col", "core")
    core_here = lax.axis_index("core")
    place = lax.axis_index("hi") * 8 + lax.axis_index("col") * 2 + core_here
    x_here = lax.axis_index("x")
    y_here = lax.axis_index("y")

    tiles = lax.all_to_all(
        feature_map.reshape(GROUP, PLANES, 16, 128), group, split_axis=0, concat_axis=0, tiled=True
    )
    share = CHANS // (X * Y)
    norms = jnp.concatenate([norm_gain, norm_bias]).reshape(1, 2 * share)
    other = lax.ppermute(norms, "y", [(0, 1), (1, 0)])
    order = jnp.stack([x_here, core_here, y_here]).astype(jnp.int32)
    scaled = call(
        scale_kernel,
        jax.ShapeDtypeStruct((16, share, LINE), BF16),
        [],
        (cotangent, jnp.broadcast_to(layer_scale[:, None, None], (share, 1, LINE))),
        1,
    )
    *mine, others = call(
        prepare_kernel,
        (jax.ShapeDtypeStruct((CHANS + 16 + 2 * share, HID), BF16),) * X + (jax.ShapeDtypeStruct((CHANS, HID), BF16),),
        [],
        (order, w_in, w_out, b_in.reshape(1, HID), norms, other, scaled),
        1,
    )
    mine = mine[:1] + [lax.ppermute(mine[step], "x", [(i, i ^ step) for i in range(X)]) for step in range(1, X)]
    others = [others] + [lax.ppermute(one, "core", [(0, 1), (1, 0)]) for one in mine[1:]]
    twins = lax.ppermute(jnp.stack([one[CHANS + 16 :] for one in mine]), "y", [(0, 1), (1, 0)])

    scale_own = own_planes(base_scale, 0, place)
    taps = tap_table(
        own_planes(base_kernel, 0, place),
        scale_own,
        own_planes(wave_kernels, 1, place),
        own_planes(wave_scale, 1, place),
    )

    def rows_of(vector):
        return over_halves(jnp.broadcast_to(vector[:, None], (PLANES, COLS)))

    layer = rows_of(own_planes(layer_scale, 0, place))
    sent = call(
        forward_kernel,
        jax.ShapeDtypeStruct((X, Y, GROUP, 2 * SUB, LINE), BF16),
        plane_scratch(),
        (tiles, taps, rows_of(scale_own * own_planes(base_bias, 0, place))),
        6,
    )
    received = lax.all_to_all(
        sent.reshape(X * Y * GROUP, 2 * SUB, LINE), everyone, split_axis=0, concat_axis=0, tiled=True
    )

    extras = jnp.stack([one[CHANS : CHANS + 6] for one in mine])
    extras = jnp.sum(extras.reshape(X, 3, 2, HID).astype(F32), 1)
    biases = extras[:, 0]
    norms = extras[:, 1].reshape(X, Y, 2, share)[x_here ^ jnp.arange(X)][:, y_here ^ jnp.arange(Y)]
    vectors = norms.transpose(2, 0, 1, 3).reshape(2, CHANS)

    anywhere = pl.BlockSpec(memory_space=pl.ANY)
    nearby = pl.BlockSpec(memory_space=pltpu.VMEM)
    blocks = (X * Y * GROUP, 4 * SUB, LINE)
    pieces = (X, GROUP // 2, 8, 16, 128)
    sent, kept, given = pl.pallas_call(
        mlp_kernel,
        out_shape=tuple(jax.ShapeDtypeStruct(shape, BF16) for shape in (blocks, pieces, pieces)),
        in_specs=[pl.BlockSpec(memory_space=pltpu.SMEM)] + [nearby] * 2 + [anywhere] * 10,
        out_specs=(anywhere,) * 3,
        scratch_shapes=[
            pltpu.VMEM(received.shape, BF16),
            pltpu.VMEM((Y, X, 2 * share, HID), BF16),
            pltpu.VMEM((X, 2, CHANS, HID), BF16),
            pltpu.VMEM((CHANS, SPOTS), F32),
            pltpu.VMEM((CHANS, SPOTS), BF16),
            pltpu.VMEM((CHANS, SPOTS), F32),
            pltpu.VMEM((CHANS, SPOTS), F32),
            pltpu.VMEM(blocks, BF16),
            pltpu.VMEM(pieces, BF16),
            pltpu.VMEM(pieces, BF16),
            pltpu.SemaphoreType.DMA((14,)),
            pltpu.SemaphoreType.DMA((12,)),
        ],
        compiler_params=pltpu.CompilerParams(vmem_limit_bytes=MLP_VMEM),
    )(
        order,
        biases,
        vectors,
        received,
        twins,
        *mine,
        *others,
    )
    received = lax.all_to_all(sent, everyone, split_axis=0, concat_axis=0, tiled=True)

    given = lax.ppermute(given, "core", [(0, 1), (1, 0)])
    parts = [summed(kept[step], given[step]) for step in range(X)]
    parts = parts[:1] + [
        lax.ppermute(parts[step], "x", [(i, i ^ step) for i in range(X)]) for step in range(1, X)
    ]

    sent = call(
        backward_kernel,
        jax.ShapeDtypeStruct((GROUP, 2 * PLANES, 16, 128), BF16),
        plane_scratch() + [pltpu.VMEM((ROWS, SUB, COLS), F32)],
        (
            received.reshape(X, Y, GROUP, 4 * SUB, LINE),
            tiles,
            taps,
            layer,
            rows_of(own_planes(b_out, 0, place)),
        ),
        6,
    )
    pieces = call(sum_kernel, jax.ShapeDtypeStruct(parts[0].shape, BF16), [], (*parts, sent[0, 0]), 1)
    pieces = lax.all_to_all(pieces, ("hi", "col"), split_axis=0, concat_axis=0, tiled=True)
    piece = summed(*[pieces[chip] for chip in range(GROUP // 2)])
    sent = jnp.concatenate([sent, jnp.broadcast_to(piece, (GROUP,) + piece.shape)], 1)
    results = lax.all_to_all(sent, group, split_axis=0, concat_axis=0, tiled=True)
    output_map, grad_map, grad_in, grad_out = call(
        finish_kernel,
        (
            jax.ShapeDtypeStruct((GROUP, PLANES, 16, 128), BF16),
            jax.ShapeDtypeStruct((GROUP, PLANES, 16, 128), BF16),
            jax.ShapeDtypeStruct((CHANS, HID), F32),
            jax.ShapeDtypeStruct((HID, CHANS), F32),
        ),
        [],
        (results, cotangent.reshape(GROUP, PLANES, 16, 128)),
        1,
    )
    output_map, grad_map = output_map.reshape(feature_map.shape), grad_map.reshape(feature_map.shape)
    return (output_map, grad_map, grad_in, grad_out)


def solution(mesh):
    grid = Mesh(mesh.devices.reshape(2, 2, 4, X, Y), ("hi", "core", "col", "x", "y"))
    chan, row = ("x", "y"), ("hi", "core")
    return jax.shard_map(
        on_device,
        mesh=grid,
        in_specs=(
            P(chan, row, "col"),
            P(chan, None, None),
            P(chan),
            P(chan),
            P(None, chan, None, None, None),
            P(None, chan, None),
            P(chan),
            P(chan),
            P(None, chan),
            P(chan),
            P(chan, None),
            P(chan),
            P(chan),
            P(chan, row, "col"),
        ),
        out_specs=(
            P(chan, row, "col"),
            P(chan, row, "col"),
            P(None, chan),
            P(chan, None),
        ),
        check_vma=False,
    )
```
